256 devices in a mesh: tm: 8 (over x, core), space: 32 (over z, y).
Axes of the slice: x: 4, y: 4, z: 8, core: 2. Of those that a mesh axis runs over, the one named last changes fastest.
Arguments:
- query_tiles: bfloat16 [8, 32, 256, 1536], P('tm', 'space'), may hold values from -100 to 100
- key_tiles: bfloat16 [8, 32, 256, 1536], P('tm', 'space'), may hold values from -4 to 4
- value_tiles: bfloat16 [8, 32, 256, 1536], P('tm', 'space'), may hold values from -6 to 6
- cotangent: bfloat16 [8, 32, 256, 1536], P('tm', 'space'), may hold values from -6 to 6
- pair_table: int32 [8, 32, 3], replicated, may hold values from -1 to 255, as said below
Outputs:
- grad_queries: bfloat16 [8, 32, 256, 1536], P('tm', 'space')
- grad_keys: bfloat16 [8, 32, 256, 1536], P('tm', 'space')
- grad_values: bfloat16 [8, 32, 256, 1536], P('tm', 'space')
The draws below stay inside these ranges and needn't reach their ends.
Inputs may be any that keep to these rules, and one draw needn't show every extreme that they name: pair_table[t, s, 0] is t * 32 + s. The following entries are distinct numbers of tiles beside (t, s): same t with s one apart, or same s with t one apart, in no fixed order; the slots after them hold -1. Some tile lists 3 tiles.
All inputs are finite; a program needn't handle non-finite values.
Results may differ from the reference program's by a relative error of at most 0.0095.
Values may be sent and summed in bfloat16 or wider, within the bound.
A program may use at most 128 MiB of HBM per device.

```python
import jax
import jax.numpy as jnp
from jax import lax

HEADS = 12
DH = 128
TILE = 256
LISTED = 3
TT = 8
TS = 32
HD = 1536


def base_keys(key):
    return jnp.clip(jax.random.normal(key, (TT, TS, TILE, HD), jnp.float32), -4.0, 4.0)


def draw_key_tiles(key, part):
    tiles = base_keys(key)
    return tiles.astype(jnp.bfloat16)


def draw_query_tiles(key, part):
    key = jax.random.fold_in(key, 5)
    tiles = jnp.clip(jax.random.normal(jax.random.fold_in(key, 1), (TT, TS, TILE, HD), jnp.float32), -4.0, 4.0)
    return tiles.astype(jnp.bfloat16)


def draw_pair_table(key, part):
    key = jax.random.fold_in(key, 9)
    time_index = lax.broadcasted_iota(jnp.int32, (TT, TS), 0)
    space_index = lax.broadcasted_iota(jnp.int32, (TT, TS), 1)
    own_number = time_index * TS + space_index
    beside = jnp.stack([own_number - TS, own_number + TS, own_number - 1, own_number + 1], axis=-1)
    inside = jnp.stack([time_index > 0, time_index < TT - 1, space_index > 0, space_index < TS - 1], axis=-1)
    face_order = jnp.arange(4, dtype=jnp.int32)
    priority = jax.random.randint(jax.random.fold_in(key, 1), (TT, TS, 4), 0, 1 << 20) * 8 + face_order
    priority = jnp.where(inside, priority, (1 << 24) + face_order)
    ranking = jnp.argsort(priority, axis=-1, stable=True)
    ordered = jnp.take_along_axis(beside, ranking, axis=-1)[:, :, :LISTED - 1]
    limit_count = jnp.minimum(jnp.sum(inside.astype(jnp.int32), axis=-1), LISTED - 1)
    listed_count = jax.random.randint(jax.random.fold_in(key, 2), (TT, TS), 0, limit_count + 1)
    forced_time = jax.random.randint(jax.random.fold_in(key, 3), (), 1, TT - 1)
    forced_space = jax.random.randint(jax.random.fold_in(key, 4), (), 1, TS - 1)
    forced = (time_index == forced_time) & (space_index == forced_space)
    listed_count = jnp.where(forced, LISTED - 1, listed_count)
    kept_slot = jnp.arange(LISTED - 1, dtype=jnp.int32) < listed_count[..., None]
    others = jnp.where(kept_slot, ordered, -1)
    return jnp.concatenate([own_number[..., None], others], axis=-1).astype(jnp.int32)


def steps_of(rng, dims, shards, smallest, high):
    loudness, own = 1.0, jax.random.fold_in(rng, 6)
    for position, parts in shards:
        draws = jnp.exp(jax.random.uniform(jax.random.fold_in(own, position), (parts,), jnp.float32, smallest / len(shards), high / len(shards)))
        loudness = loudness * jnp.repeat(draws, dims[position] // parts).reshape([-1 if axis == position else 1 for axis in range(len(dims))])
    return loudness


def scatter_about(stream_key, dims, scale, limit, pieces=(), kind=jnp.bfloat16):
    array = jax.random.normal(stream_key, dims, jnp.float32) * scale
    if len(pieces) > 0:
        array = steps_of(stream_key, dims, pieces, -0.22, 0.18) * array
    return jnp.clip(array, min=-limit, max=limit).astype(kind)


def setup_inputs(seed: int = 0) -> dict:
    arg_keys = jax.random.split(jax.random.key(seed), 6)
    return {
        "query_tiles": draw_query_tiles(jax.random.fold_in(arg_keys[5], 71), 0),
        "key_tiles": draw_key_tiles(jax.random.fold_in(arg_keys[5], 71), 0),
        "value_tiles": scatter_about(arg_keys[2], (TT, TS, TILE, HD), 1.0, 6.0, ((0, 8), (1, 32))),
        "cotangent": scatter_about(arg_keys[3], (TT, TS, TILE, HD), 1.0, 6.0, ((0, 8), (1, 32))),
        "pair_table": draw_pair_table(jax.random.fold_in(arg_keys[5], 71), 0),
    }


def rounded(tensor):
    return lax.optimization_barrier(tensor.astype(jnp.bfloat16)).astype(jnp.float32)


def reference(query_tiles, key_tiles, value_tiles, cotangent, pair_table):
    tile_count = TT * TS
    score_scale = DH ** -0.5
    query_flat = query_tiles.reshape(tile_count, TILE, HEADS, DH)
    key_flat = key_tiles.reshape(tile_count, TILE, HEADS, DH)
    value_flat = value_tiles.reshape(tile_count, TILE, HEADS, DH)
    grad_flat = cotangent.reshape(tile_count, TILE, HEADS, DH)
    listing_flat = pair_table.reshape(tile_count, LISTED)
    first_slot = jnp.arange(LISTED, dtype=jnp.int32) == 0

    def tile_step(carried, tile_number):
        key_total, value_total = carried
        listing = listing_flat[tile_number]
        is_listed = listing >= 0
        safe_number = jnp.where(is_listed, listing, 0).astype(jnp.int32)
        key_rows = key_flat[safe_number].astype(jnp.float32)
        value_rows = value_flat[safe_number].astype(jnp.float32)
        query_rows = query_flat[tile_number].astype(jnp.float32)
        grad_rows = grad_flat[tile_number].astype(jnp.float32)
        scores = jnp.einsum("qhd,lkhd->hqlk", query_rows, key_rows) * score_scale
        scores = jnp.where(is_listed[None, None, :, None], scores, -jnp.inf)
        row_peak = jnp.max(scores, axis=(2, 3), keepdims=True)
        log_norm = row_peak + jnp.log(jnp.sum(jnp.exp(scores - row_peak), axis=(2, 3), keepdims=True))
        weights = rounded(jnp.exp(scores - log_norm))
        attended = jnp.einsum("hqlk,lkhd->qhd", weights, value_rows)
        row_delta = jnp.sum(grad_rows * attended, axis=-1).T
        weight_grads = jnp.einsum("qhd,lkhd->hqlk", grad_rows, value_rows)
        score_grads = rounded(weights * (weight_grads - row_delta[:, :, None, None]) * score_scale)
        grad_query = jnp.einsum("hqlk,lkhd->qhd", score_grads, key_rows).astype(jnp.bfloat16)
        key_terms = jnp.einsum("hqlk,qhd->lkhd", score_grads, query_rows)
        value_terms = jnp.einsum("hqlk,qhd->lkhd", weights, grad_rows)
        key_terms = jnp.where(first_slot[:, None, None, None], key_terms, rounded(key_terms))
        value_terms = jnp.where(first_slot[:, None, None, None], value_terms, rounded(value_terms))
        target = jnp.where(is_listed, listing, tile_count).astype(jnp.int32)
        key_total = key_total.at[target].add(key_terms, mode="drop")
        value_total = value_total.at[target].add(value_terms, mode="drop")
        return (key_total, value_total), grad_query

    zeroed = jnp.zeros((tile_count, TILE, HEADS, DH), jnp.float32)
    (key_total, value_total), grad_stack = lax.scan(tile_step, (zeroed, zeroed), jnp.arange(tile_count, dtype=jnp.int32))
    out_shape = (TT, TS, TILE, HEADS * DH)
    return (grad_stack.reshape(out_shape), key_total.reshape(out_shape).astype(jnp.bfloat16), value_total.reshape(out_shape).astype(jnp.bfloat16))
```

```python
import functools
import math

import jax
import jax.numpy as jnp
from jax import lax
from jax.experimental import pallas as pl
from jax.experimental.pallas import tpu as pltpu
from jax.sharding import PartitionSpec as P

HEADS = 12
AHEAD = 3
FAR = -1e30
MESH = pl.DeviceIdType.MESH
OPPOSITE = (1, 0, 3, 2)
NT = (((1,), (1,)), ((), ()))
NN = (((1,), (0,)), ((), ()))


def dot(a, b, dims):
    return lax.dot_general(a, b, dims, preferred_element_type=jnp.float32)


def kernel(
    span_time, span_space, rows, size,
    table, q_hbm, k_hbm, v_hbm, g_hbm,
    dq_out, dk_out, dv_out,
    q_own, k_own, v_own, g_own, near, p_kept, dp_kept,
    stat_own, stat_out, stat_in, fin_own, fin_out, fin_in,
    ret_out, ret_in, dq_own,
    load_sem, near_send, near_recv, stat_send, stat_recv, fin_send, fin_recv, ret_send, ret_recv,
):
    t = lax.axis_index("tm")
    s = lax.axis_index("space")
    faces = (
        ((t - 1, s), t > 0, -span_space),
        ((t + 1, s), t < span_time - 1, span_space),
        ((t, s - 1), s > 0, -1),
        ((t, s + 1), s < span_space - 1, 1),
    )
    order = (2, 3, 0, 1)
    scale = size ** (-0.5)
    to_exp2 = scale * math.log2(math.e)

    loads = [
        pltpu.make_async_copy(src.at[0, 0], dst, load_sem.at[i])
        for i, (src, dst) in enumerate(((q_hbm, q_own), (k_hbm, k_own), (v_hbm, v_own), (g_hbm, g_own)))
    ]
    for load in loads:
        load.start()

    barrier = pltpu.get_barrier_semaphore()
    for device, there, _ in faces:
        @pl.when(there)
        def _(device=device):
            pl.semaphore_signal(barrier, 1, device_id=device, device_id_type=MESH)
    pl.semaphore_wait(barrier, sum(there.astype(jnp.int32) for _, there, _ in faces))

    def columns(h):
        return pl.ds(pl.multiple_of(h * size, size), size)

    def near_copies(h, f):
        return [
            pltpu.make_async_remote_copy(
                src.at[0, 0, :, columns(h)], near.at[OPPOSITE[f], u, h],
                near_send.at[f, u, h], near_recv.at[OPPOSITE[f], u, h],
                device_id=faces[f][0], device_id_type=MESH,
            )
            for u, src in enumerate((q_hbm, g_hbm))
        ]

    def face_copy(out, arrived, send, recv, h, f):
        return pltpu.make_async_remote_copy(
            out.at[f, h], arrived.at[OPPOSITE[f], h], send.at[f, h], recv.at[OPPOSITE[f], h],
            device_id=faces[f][0], device_id_type=MESH,
        )

    def arrival(arrived, send, recv, h, f):
        return pltpu.make_async_remote_copy(
            arrived.at[f, h], arrived.at[f, h], send.at[f, h], recv.at[f, h],
            device_id=faces[f][0], device_id_type=MESH,
        )

    def send_near(h):
        for f in order:
            @pl.when(faces[f][1])
            def _(f=f):
                for copy in near_copies(h, f):
                    copy.start()

    def start_first(h, carry):
        send_near(h)
        return carry

    lax.fori_loop(0, AHEAD, start_first, 0)

    for f in range(4):
        @pl.when(jnp.logical_not(faces[f][1]))
        def _(f=f):
            def clear(h, carry):
                near[f, 0, h] = jnp.zeros((rows, size), jnp.bfloat16)
                near[f, 1, h] = jnp.zeros((rows, size), jnp.bfloat16)
                fin_in[f, h] = jnp.zeros((8, rows), jnp.float32)
                ret_in[f, h] = jnp.zeros((size, rows), jnp.bfloat16)
                return carry

            lax.fori_loop(0, HEADS, clear, 0)

    for load in loads:
        load.wait()

    number = t * span_space + s
    first, second = table[t, s, 1], table[t, s, 2]
    listed = [
        jnp.logical_or(first == number + by, second == number + by) for _, _, by in faces
    ]

    def query_side(h, j):
        if j == 4:
            return q_own[:, columns(h)], g_own[:, columns(h)]
        return near[j, 0, h], near[j, 1, h]

    def score_step(h):
        slot = lax.rem(h, 3)
        for f in order:
            @pl.when(faces[f][1])
            def _(f=f):
                for u in range(2):
                    pltpu.make_async_remote_copy(
                        near.at[f, u, h], near.at[f, u, h], near_send.at[f, u, h], near_recv.at[f, u, h],
                        device_id=faces[f][0], device_id_type=MESH,
                    ).wait_recv()
        keys, values = k_own[:, columns(h)], v_own[:, columns(h)]
        for j in (2, 3, 0, 1, 4):
            queries, grads = query_side(h, j)
            scores = dot(keys, queries, NT)
            peak = jnp.max(scores, axis=0, keepdims=True)
            p = jnp.exp2((scores - peak) * to_exp2)
            dp = dot(values, grads, NT)
            p_kept[slot, j] = p
            dp_kept[slot, j] = dp
            total = jnp.sum(p, axis=0, keepdims=True)
            delta = jnp.sum(p * dp, axis=0, keepdims=True)
            target = stat_own.at[slot] if j == 4 else stat_out.at[j, h]
            target[0:1, :] = peak
            target[1:2, :] = total
            target[2:3, :] = delta
            if j < 4:
                @pl.when(faces[j][1])
                def _(j=j):
                    face_copy(stat_out, stat_in, stat_send, stat_recv, h, j).start()

    def norm_step(h):
        slot = lax.rem(h, 3)
        for f in order:
            @pl.when(faces[f][1])
            def _(f=f):
                arrival(stat_in, stat_send, stat_recv, h, f).wait_recv()
        peaks, totals, deltas = [], [], []
        for f in range(4):
            peaks.append(jnp.where(listed[f], stat_in[f, h, 0:1, :], FAR))
            totals.append(jnp.where(listed[f], stat_in[f, h, 1:2, :], 0.0))
            deltas.append(jnp.where(listed[f], stat_in[f, h, 2:3, :], 0.0))
        peaks.append(stat_own[slot, 0:1, :])
        totals.append(stat_own[slot, 1:2, :])
        deltas.append(stat_own[slot, 2:3, :])
        peak = functools.reduce(jnp.maximum, peaks)
        shares = [jnp.exp2((part - peak) * to_exp2) for part in peaks]
        total = functools.reduce(jnp.add, [a * b for a, b in zip(shares, totals)])
        delta = functools.reduce(jnp.add, [a * b for a, b in zip(shares, deltas)])
        inverse = 1.0 / total
        delta = delta * inverse
        for f in range(5):
            target = fin_own.at[slot] if f == 4 else fin_out.at[f, h]
            target[0:1, :] = shares[f] * inverse
            target[1:2, :] = delta
        for f in order:
            @pl.when(faces[f][1])
            def _(f=f):
                face_copy(fin_out, fin_in, fin_send, fin_recv, h, f).start()

    def grad_step(h):
        slot = lax.rem(h, 3)
        for f in order:
            @pl.when(faces[f][1])
            def _(f=f):
                arrival(fin_in, fin_send, fin_recv, h, f).wait_recv()
        keys_t = k_own[:, columns(h)].T
        dk = jnp.zeros((rows, size), jnp.float32)
        dv = jnp.zeros((rows, size), jnp.float32)
        for j in (2, 3, 0, 1, 4):
            queries, grads = query_side(h, j)
            fin = fin_own.at[slot] if j == 4 else fin_in.at[j, h]
            weights = (p_kept[slot, j] * fin[0:1, :]).astype(jnp.bfloat16)
            ds = (weights.astype(jnp.float32) * (dp_kept[slot, j] - fin[1:2, :])).astype(jnp.bfloat16)
            dv += dot(weights, grads, NN)
            dk += dot(ds, queries, NN)
            dq = dot(keys_t, ds, NN) * scale
            if j == 4:
                dq_own[h] = dq
            else:
                ret_out[j, h] = dq.astype(jnp.bfloat16)

                @pl.when(faces[j][1])
                def _(j=j):
                    face_copy(ret_out, ret_in, ret_send, ret_recv, h, j).start()
        dk_out[0, 0, :, columns(h)] = (dk * scale).astype(jnp.bfloat16)
        dv_out[0, 0, :, columns(h)] = dv.astype(jnp.bfloat16)

    def query_step(h):
        for f in order:
            @pl.when(faces[f][1])
            def _(f=f):
                arrival(ret_in, ret_send, ret_recv, h, f).wait_recv()
        total = dq_own[h]
        for f in range(4):
            total += ret_in[f, h].astype(jnp.float32)
        dq_out[0, 0, :, columns(h)] = total.T.astype(jnp.bfloat16)

    late = 5

    def step(i, carry):
        @pl.when(i + AHEAD < HEADS)
        def _():
            send_near(i + AHEAD)

        @pl.when(jnp.logical_and(i >= 2, i < HEADS + 2))
        def _():
            grad_step(i - 2)

        @pl.when(i < HEADS)
        def _():
            score_step(i)

        @pl.when(jnp.logical_and(i >= 1, i < HEADS + 1))
        def _():
            norm_step(i - 1)

        @pl.when(i >= late)
        def _():
            query_step(i - late)

        return carry

    lax.fori_loop(0, HEADS + late, step, 0)

    def drain(h, carry):
        for f in range(4):
            @pl.when(faces[f][1])
            def _(f=f):
                for copy in near_copies(h, f):
                    copy.wait_send()
                face_copy(stat_out, stat_in, stat_send, stat_recv, h, f).wait_send()
                face_copy(fin_out, fin_in, fin_send, fin_recv, h, f).wait_send()
                face_copy(ret_out, ret_in, ret_send, ret_recv, h, f).wait_send()
        return carry

    lax.fori_loop(0, HEADS, drain, 0)


def solution(mesh):
    span_time, span_space = mesh.shape["tm"], mesh.shape["space"]

    def per_device(query_tiles, key_tiles, value_tiles, cotangent, pair_table):
        shape = query_tiles.shape
        rows, width = shape[2], shape[3]
        size = width // HEADS
        out = jax.ShapeDtypeStruct(shape, jnp.bfloat16)
        half, full = jnp.bfloat16, jnp.float32
        dma = pltpu.SemaphoreType.DMA
        return pl.pallas_call(
            functools.partial(kernel, span_time, span_space, rows, size),
            out_shape=(out, out, out),
            in_specs=[pl.BlockSpec(memory_space=pltpu.SMEM)]
            + [pl.BlockSpec(memory_space=pl.ANY)] * 4,
            out_specs=[pl.BlockSpec(memory_space=pltpu.VMEM)] * 3,
            scratch_shapes=[
                pltpu.VMEM((rows, width), half),
                pltpu.VMEM((rows, width), half),
                pltpu.VMEM((rows, width), half),
                pltpu.VMEM((rows, width), half),
                pltpu.VMEM((4, 2, HEADS, rows, size), half),
                pltpu.VMEM((3, 5, rows, rows), full),
                pltpu.VMEM((3, 5, rows, rows), full),
                pltpu.VMEM((3, 8, rows), full),
                pltpu.VMEM((4, HEADS, 8, rows), full),
                pltpu.VMEM((4, HEADS, 8, rows), full),
                pltpu.VMEM((3, 8, rows), full),
                pltpu.VMEM((4, HEADS, 8, rows), full),
                pltpu.VMEM((4, HEADS, 8, rows), full),
                pltpu.VMEM((4, HEADS, size, rows), half),
                pltpu.VMEM((4, HEADS, size, rows), half),
                pltpu.VMEM((HEADS, size, rows), full),
                dma((4,)),
                dma((4, 2, HEADS)),
                dma((4, 2, HEADS)),
            ]
            + [dma((4, HEADS))] * 6,
            compiler_params=pltpu.CompilerParams(
                collective_id=0, has_side_effects=True, vmem_limit_bytes=50 << 20
            ),
            cost_estimate=pl.CostEstimate(
                flops=5 * 5 * 2 * rows * rows * width, bytes_accessed=14 * rows * width, transcendentals=5 * HEADS * rows * rows
            ),
        )(pair_table, query_tiles, key_tiles, value_tiles, cotangent)

    tile = P("tm", "space", None, None)
    return jax.shard_map(
        per_device, mesh=mesh, in_specs=(tile, tile, tile, tile, P()), out_specs=(tile, tile, tile), check_vma=False
    )
```

```python
import functools
import math

import jax
import jax.numpy as jnp
from jax import lax
from jax.experimental import pallas as pl
from jax.experimental.pallas import tpu as pltpu
from jax.sharding import PartitionSpec as P

HEADS = 12
NORM_LAG, GRAD_LAG, QUERY_LAG = 2, 4, 7
SLOTS = GRAD_LAG + 1
ROUNDS = 12
AHEAD = 3
FAR = -1e30
MESH = pl.DeviceIdType.MESH
OPPOSITE = (1, 0, 3, 2)
NT = (((1,), (1,)), ((), ()))
NN = (((1,), (0,)), ((), ()))


def dot(a, b, dims):
    return lax.dot_general(a, b, dims, preferred_element_type=jnp.float32)


def kernel(
    span_time, span_space, rows, size,
    table, q_hbm, k_hbm, v_hbm, g_hbm,
    dq_out, dk_out, dv_out,
    q_own, k_own, v_own, g_own, near, p_kept, dp_kept, inv_kept,
    stat_own, stat_out, stat_in, fin_own, fin_out, fin_in,
    ret_out, ret_in, dq_own,
    load_sem, near_send, near_recv, stat_send, stat_recv, fin_send, fin_recv, ret_send, ret_recv,
):
    t = lax.axis_index("tm")
    s = lax.axis_index("space")
    faces = (
        ((t - 1, s), t > 0, -span_space),
        ((t + 1, s), t < span_time - 1, span_space),
        ((t, s - 1), s > 0, -1),
        ((t, s + 1), s < span_space - 1, 1),
    )
    order = (2, 3, 0, 1)
    scale = size ** (-0.5)
    to_exp2 = scale * math.log2(math.e)

    loads = [
        pltpu.make_async_copy(src.at[0, 0], dst, load_sem.at[i])
        for i, (src, dst) in enumerate(((q_hbm, q_own), (k_hbm, k_own), (v_hbm, v_own), (g_hbm, g_own)))
    ]
    for load in loads:
        load.start()

    barrier = pltpu.get_barrier_semaphore()
    for device, there, _ in faces:
        @pl.when(there)
        def _(device=device):
            pl.semaphore_signal(barrier, 1, device_id=device, device_id_type=MESH)
    pl.semaphore_wait(barrier, sum(there.astype(jnp.int32) for _, there, _ in faces))

    def columns(h):
        return pl.ds(pl.multiple_of(h * size, size), size)

    def near_copies(h, f):
        return [
            pltpu.make_async_remote_copy(
                src.at[0, 0, :, columns(h)], near.at[OPPOSITE[f], h, u],
                near_send.at[f], near_recv.at[OPPOSITE[f], lax.rem(h, ROUNDS)],
                device_id=faces[f][0], device_id_type=MESH,
            )
            for u, src in enumerate((q_hbm, g_hbm))
        ]

    def face_copy(out, arrived, send, recv, h, f):
        return pltpu.make_async_remote_copy(
            out.at[f, h], arrived.at[OPPOSITE[f], h], send.at[f], recv.at[OPPOSITE[f], lax.rem(h, ROUNDS)],
            device_id=faces[f][0], device_id_type=MESH,
        )

    def arrival(arrived, send, recv, h, f):
        return pltpu.make_async_remote_copy(
            arrived.at[f, h], arrived.at[f, h], send.at[f], recv.at[f, lax.rem(h, ROUNDS)],
            device_id=faces[f][0], device_id_type=MESH,
        )

    def send_near(h):
        for f in order:
            @pl.when(faces[f][1])
            def _(f=f):
                for copy in near_copies(h, f):
                    copy.start()

    def start_first(h, carry):
        send_near(h)
        return carry

    lax.fori_loop(0, AHEAD, start_first, 0)

    for f in range(4):
        @pl.when(jnp.logical_not(faces[f][1]))
        def _(f=f):
            def clear(h, carry):
                near[f, h] = jnp.zeros((2, rows, size), jnp.bfloat16)
                fin_in[f, h] = jnp.zeros((4, rows // 2), jnp.float32)
                ret_in[f, h] = jnp.zeros((size, rows), jnp.bfloat16)
                return carry

            lax.fori_loop(0, HEADS, clear, 0)

    for load in loads:
        load.wait()

    number = t * span_space + s
    first, second = table[1, t, s], table[2, t, s]
    listed = [
        jnp.logical_or(first == number + by, second == number + by) for _, _, by in faces
    ]

    def put_rows(target, upper, lower):
        half = rows // 2
        target[0:1, :] = upper[:, :half]
        target[1:2, :] = upper[:, half:]
        target[2:3, :] = lower[:, :half]
        target[3:4, :] = lower[:, half:]

    def get_rows(source):
        upper = jnp.concatenate([source[0:1, :], source[1:2, :]], axis=1)
        lower = jnp.concatenate([source[2:3, :], source[3:4, :]], axis=1)
        return upper, lower

    def query_side(h, j):
        if j == 4:
            return q_own[:, columns(h)], g_own[:, columns(h)]
        return near[j, h, 0], near[j, h, 1]

    def score_step(h):
        slot = lax.rem(h, SLOTS)
        for f in order:
            @pl.when(faces[f][1])
            def _(f=f):
                arrival(near, near_send, near_recv, h, f).wait_recv()
        keys, values = k_own[:, columns(h)], v_own[:, columns(h)]
        for j in (2, 3, 0, 1, 4):
            queries, grads = query_side(h, j)
            scores = dot(keys, queries, NT)
            peak = jnp.max(scores, axis=0, keepdims=True)
            p = jnp.exp2((scores - peak) * to_exp2)
            dp = dot(values, grads, NT)
            p_kept[slot, j] = p
            dp_kept[slot, j] = dp
            total = jnp.sum(p, axis=0, keepdims=True)
            inverse = 1.0 / total
            delta = jnp.sum(p * dp, axis=0, keepdims=True) * inverse
            inv_kept[slot, j] = inverse
            put_rows(stat_own.at[slot] if j == 4 else stat_out.at[j, h], peak * to_exp2 + jnp.log2(total), delta)
        for f in order:
            @pl.when(faces[f][1])
            def _(f=f):
                face_copy(stat_out, stat_in, stat_send, stat_recv, h, f).start()

    def norm_step(h):
        slot = lax.rem(h, SLOTS)
        for f in order:
            @pl.when(faces[f][1])
            def _(f=f):
                arrival(stat_in, stat_send, stat_recv, h, f).wait_recv()
        norms, deltas = [], []
        for f in range(4):
            norms.append(jnp.where(listed[f], stat_in[f, h, 0:2, :], FAR))
            deltas.append(jnp.where(listed[f], stat_in[f, h, 2:4, :], 0.0))
        norms.append(stat_own[slot, 0:2, :])
        deltas.append(stat_own[slot, 2:4, :])
        peak = functools.reduce(jnp.maximum, norms)
        shares = [jnp.exp2(norm - peak) for norm in norms]
        inverse = 1.0 / functools.reduce(jnp.add, shares)
        shares = [share * inverse for share in shares]
        delta = functools.reduce(jnp.add, [a * b for a, b in zip(shares, deltas)])
        for f in range(5):
            target = fin_own.at[slot] if f == 4 else fin_out.at[f, h]
            target[0:2, :] = shares[f]
            target[2:4, :] = delta
        for f in order:
            @pl.when(faces[f][1])
            def _(f=f):
                face_copy(fin_out, fin_in, fin_send, fin_recv, h, f).start()

    def grad_step(h):
        slot = lax.rem(h, SLOTS)
        for f in order:
            @pl.when(faces[f][1])
            def _(f=f):
                arrival(fin_in, fin_send, fin_recv, h, f).wait_recv()
        keys_t = k_own[:, columns(h)].T
        dk = jnp.zeros((rows, size), jnp.float32)
        dv = jnp.zeros((rows, size), jnp.float32)
        for j in (2, 3, 0, 1, 4):
            queries, grads = query_side(h, j)
            share, delta = get_rows(fin_own.at[slot] if j == 4 else fin_in.at[j, h])
            weights = (p_kept[slot, j] * (share * inv_kept[slot, j])).astype(jnp.bfloat16)
            ds = (weights.astype(jnp.float32) * (dp_kept[slot, j] - delta)).astype(jnp.bfloat16)
            dv += dot(weights, grads, NN)
            dk += dot(ds, queries, NN)
            dq = dot(keys_t, ds, NN) * scale
            if j == 4:
                dq_own[h] = dq
            else:
                ret_out[j, h] = dq.astype(jnp.bfloat16)
        dk_out[0, 0, :, columns(h)] = (dk * scale).astype(jnp.bfloat16)
        dv_out[0, 0, :, columns(h)] = dv.astype(jnp.bfloat16)
        for f in order:
            @pl.when(faces[f][1])
            def _(f=f):
                face_copy(ret_out, ret_in, ret_send, ret_recv, h, f).start()

    def query_step(h):
        for f in order:
            @pl.when(faces[f][1])
            def _(f=f):
                arrival(ret_in, ret_send, ret_recv, h, f).wait_recv()
        total = dq_own[h]
        for f in range(4):
            total += ret_in[f, h].astype(jnp.float32)
        dq_out[0, 0, :, columns(h)] = total.T.astype(jnp.bfloat16)

    def step(i, carry):
        @pl.when(i < HEADS)
        def _():
            score_step(i)

        @pl.when(jnp.logical_and(i >= NORM_LAG, i < HEADS + NORM_LAG))
        def _():
            norm_step(i - NORM_LAG)

        @pl.when(jnp.logical_and(i >= GRAD_LAG, i < HEADS + GRAD_LAG))
        def _():
            grad_step(i - GRAD_LAG)

        @pl.when(i + AHEAD < HEADS)
        def _():
            send_near(i + AHEAD)

        @pl.when(i >= QUERY_LAG)
        def _():
            query_step(i - QUERY_LAG)

        return carry

    lax.fori_loop(0, HEADS + QUERY_LAG, step, 0)

    for f in range(4):
        @pl.when(faces[f][1])
        def _(f=f):
            for out, send in ((near, near_send), (stat_out, stat_send), (fin_out, fin_send), (ret_out, ret_send)):
                pltpu.make_async_remote_copy(
                    out.at[f], out.at[f], send.at[f], near_recv.at[f, 0], device_id=faces[f][0], device_id_type=MESH
                ).wait_send()


def hand_over(a, b, c, x, y, z, sem):
    copies = [pltpu.make_async_copy(p, q, sem.at[i]) for i, (p, q) in enumerate(((a, x), (b, y), (c, z)))]
    for copy in copies:
        copy.start()
    for copy in copies:
        copy.wait()


def solution(mesh):
    span_time, span_space = mesh.shape["tm"], mesh.shape["space"]

    def per_device(query_tiles, key_tiles, value_tiles, cotangent, pair_table):
        shape = query_tiles.shape
        rows, width = shape[2], shape[3]
        size = width // HEADS
        out = jax.ShapeDtypeStruct(shape, jnp.bfloat16)
        half, full = jnp.bfloat16, jnp.float32
        dma = pltpu.SemaphoreType.DMA
        results = pl.pallas_call(
            functools.partial(kernel, span_time, span_space, rows, size),
            out_shape=(out, out, out),
            in_specs=[pl.BlockSpec(memory_space=pltpu.SMEM)]
            + [pl.BlockSpec(memory_space=pl.ANY)] * 4,
            out_specs=[pl.BlockSpec(memory_space=pltpu.VMEM)] * 3,
            scratch_shapes=[
                pltpu.VMEM((rows, width), half),
                pltpu.VMEM((rows, width), half),
                pltpu.VMEM((rows, width), half),
                pltpu.VMEM((rows, width), half),
                pltpu.VMEM((4, HEADS, 2, rows, size), half),
                pltpu.VMEM((SLOTS, 5, rows, rows), full),
                pltpu.VMEM((SLOTS, 5, rows, rows), full),
                pltpu.VMEM((SLOTS, 5, 1, rows), full),
                pltpu.VMEM((SLOTS, 4, rows // 2), full),
                pltpu.VMEM((4, HEADS, 4, rows // 2), full),
                pltpu.VMEM((4, HEADS, 4, rows // 2), full),
                pltpu.VMEM((SLOTS, 4, rows // 2), full),
                pltpu.VMEM((4, HEADS, 4, rows // 2), full),
                pltpu.VMEM((4, HEADS, 4, rows // 2), full),
                pltpu.VMEM((4, HEADS, size, rows), half),
                pltpu.VMEM((4, HEADS, size, rows), half),
                pltpu.VMEM((HEADS, size, rows), full),
                dma((4,)),
            ]
            + [dma((4,)), dma((4, ROUNDS))] * 4,
            compiler_params=pltpu.CompilerParams(
                collective_id=0, has_side_effects=True, vmem_limit_bytes=51 << 20
            ),
            cost_estimate=pl.CostEstimate(
                flops=5 * 5 * 2 * rows * rows * width, bytes_accessed=14 * rows * width, transcendentals=5 * HEADS * rows * rows
            ),
        )(pair_table.transpose(2, 0, 1), query_tiles, key_tiles, value_tiles, cotangent)
        return pl.pallas_call(
            hand_over,
            out_shape=(out, out, out),
            in_specs=[pl.BlockSpec(memory_space=pl.ANY)] * 3,
            out_specs=[pl.BlockSpec(memory_space=pl.ANY)] * 3,
            scratch_shapes=[dma((3,))],
            compiler_params=pltpu.CompilerParams(vmem_limit_bytes=1 << 20),
        )(*results)

    tile = P("tm", "space", None, None)
    return jax.shard_map(
        per_device, mesh=mesh, in_specs=(tile, tile, tile, tile, P()), out_specs=(tile, tile, tile), check_vma=False
    )
```

```python
import functools
import math

import jax
import jax.numpy as jnp
from jax import lax
from jax.experimental import pallas as pl
from jax.experimental.pallas import tpu as pltpu
from jax.sharding import PartitionSpec as P

HEADS = 12
NORM_LAG, GRAD_LAG, QUERY_LAG = 3, 6, 9
SLOTS = GRAD_LAG + 1
ROUNDS = 8
AHEAD = 4
FAR = -1e30
MESH = pl.DeviceIdType.MESH
OPPOSITE = (1, 0, 3, 2)
NT = (((1,), (1,)), ((), ()))
NN = (((1,), (0,)), ((), ()))


def dot(a, b, dims):
    return lax.dot_general(a, b, dims, preferred_element_type=jnp.float32)


def kernel(
    span_time, span_space, rows, size,
    table_hbm, q_hbm, k_hbm, v_hbm, g_hbm,
    dq_out, dk_out, dv_out,
    table, q_own, k_own, v_own, g_own, near, p_kept, dp_kept, inv_kept,
    stat_own, stat_out, stat_in, fin_own, fin_out, fin_in,
    ret_out, ret_in, dq_own,
    load_sem, near_send, near_recv, stat_send, stat_recv, fin_send, fin_recv, ret_send, ret_recv,
):
    t = lax.axis_index("tm")
    s = lax.axis_index("space")
    faces = (
        ((t - 1, s), t > 0, -span_space),
        ((t + 1, s), t < span_time - 1, span_space),
        ((t, s - 1), s > 0, -1),
        ((t, s + 1), s < span_space - 1, 1),
    )
    order = (2, 3, 0, 1)
    scale = size ** (-0.5)
    to_exp2 = scale * math.log2(math.e)

    loads = [
        pltpu.make_async_copy(src.at[0, 0], dst, load_sem.at[i])
        for i, (src, dst) in enumerate(((q_hbm, q_own), (k_hbm, k_own), (v_hbm, v_own), (g_hbm, g_own)))
    ]
    loads.append(pltpu.make_async_copy(table_hbm, table, load_sem.at[4]))
    for load in loads:
        load.start()

    barrier = pltpu.get_barrier_semaphore()
    for device, there, _ in faces:
        @pl.when(there)
        def _(device=device):
            pl.semaphore_signal(barrier, 1, device_id=device, device_id_type=MESH)
    pl.semaphore_wait(barrier, sum(there.astype(jnp.int32) for _, there, _ in faces))

    def columns(h):
        return pl.ds(pl.multiple_of(h * size, size), size)

    def near_copies(h, f):
        return [
            pltpu.make_async_remote_copy(
                src.at[0, 0, :, columns(h)], near.at[OPPOSITE[f], h, u],
                near_send.at[f], near_recv.at[OPPOSITE[f], lax.rem(h, ROUNDS)],
                device_id=faces[f][0], device_id_type=MESH,
            )
            for u, src in enumerate((q_hbm, g_hbm))
        ]

    def face_copy(out, arrived, send, recv, h, f):
        return pltpu.make_async_remote_copy(
            out.at[f, h], arrived.at[OPPOSITE[f], h], send.at[f], recv.at[OPPOSITE[f], lax.rem(h, ROUNDS)],
            device_id=faces[f][0], device_id_type=MESH,
        )

    def arrival(arrived, send, recv, h, f):
        return pltpu.make_async_remote_copy(
            arrived.at[f, h], arrived.at[f, h], send.at[f], recv.at[f, lax.rem(h, ROUNDS)],
            device_id=faces[f][0], device_id_type=MESH,
        )

    def send_near(h):
        for f in order:
            @pl.when(faces[f][1])
            def _(f=f):
                for copy in near_copies(h, f):
                    copy.start()

    def start_first(h, carry):
        send_near(h)
        return carry

    lax.fori_loop(0, AHEAD, start_first, 0)

    for f in range(4):
        @pl.when(jnp.logical_not(faces[f][1]))
        def _(f=f):
            def clear(h, carry):
                near[f, h] = jnp.zeros((2, rows, size), jnp.bfloat16)
                fin_in[f, h] = jnp.zeros((4, rows // 2), jnp.float32)
                ret_in[f, h] = jnp.zeros((size, rows), jnp.bfloat16)
                return carry

            lax.fori_loop(0, HEADS, clear, 0)

    for load in loads:
        load.wait()

    number = t * span_space + s
    first, second = table[1, t, s], table[2, t, s]
    listed = [
        jnp.logical_or(first == number + by, second == number + by) for _, _, by in faces
    ]

    def put_rows(target, upper, lower):
        half = rows // 2
        target[0:1, :] = upper[:, :half]
        target[1:2, :] = upper[:, half:]
        target[2:3, :] = lower[:, :half]
        target[3:4, :] = lower[:, half:]

    def get_rows(source):
        upper = jnp.concatenate([source[0:1, :], source[1:2, :]], axis=1)
        lower = jnp.concatenate([source[2:3, :], source[3:4, :]], axis=1)
        return upper, lower

    def query_side(h, j):
        if j == 4:
            return q_own[:, columns(h)], g_own[:, columns(h)]
        return near[j, h, 0], near[j, h, 1]

    def score_step(h):
        slot = lax.rem(h, SLOTS)
        for f in order:
            @pl.when(faces[f][1])
            def _(f=f):
                arrival(near, near_send, near_recv, h, f).wait_recv()
        keys, values = k_own[:, columns(h)], v_own[:, columns(h)]
        for j in (2, 3, 0, 1, 4):
            queries, grads = query_side(h, j)
            scores = dot(keys, queries, NT)
            peak = jnp.max(scores, axis=0, keepdims=True)
            p = jnp.exp2((scores - peak) * to_exp2)
            dp = dot(values, grads, NT)
            p_kept[slot, j] = p
            dp_kept[slot, j] = dp
            total = jnp.sum(p, axis=0, keepdims=True)
            inverse = 1.0 / total
            delta = jnp.sum(p * dp, axis=0, keepdims=True) * inverse
            inv_kept[slot, j] = inverse
            put_rows(stat_own.at[slot] if j == 4 else stat_out.at[j, h], peak * to_exp2 + jnp.log2(total), delta)
        for f in order:
            @pl.when(faces[f][1])
            def _(f=f):
                face_copy(stat_out, stat_in, stat_send, stat_recv, h, f).start()

    def norm_step(h):
        slot = lax.rem(h, SLOTS)
        for f in order:
            @pl.when(faces[f][1])
            def _(f=f):
                arrival(stat_in, stat_send, stat_recv, h, f).wait_recv()
        norms, deltas = [], []
        for f in range(4):
            norms.append(jnp.where(listed[f], stat_in[f, h, 0:2, :], FAR))
            deltas.append(jnp.where(listed[f], stat_in[f, h, 2:4, :], 0.0))
        norms.append(stat_own[slot, 0:2, :])
        deltas.append(stat_own[slot, 2:4, :])
        peak = functools.reduce(jnp.maximum, norms)
        shares = [jnp.exp2(norm - peak) for norm in norms]
        inverse = 1.0 / functools.reduce(jnp.add, shares)
        shares = [share * inverse for share in shares]
        delta = functools.reduce(jnp.add, [a * b for a, b in zip(shares, deltas)])
        for f in range(5):
            target = fin_own.at[slot] if f == 4 else fin_out.at[f, h]
            target[0:2, :] = shares[f]
            target[2:4, :] = delta
        for f in order:
            @pl.when(faces[f][1])
            def _(f=f):
                face_copy(fin_out, fin_in, fin_send, fin_recv, h, f).start()

    def grad_step(h):
        slot = lax.rem(h, SLOTS)
        for f in order:
            @pl.when(faces[f][1])
            def _(f=f):
                arrival(fin_in, fin_send, fin_recv, h, f).wait_recv()
        keys_t = k_own[:, columns(h)].T
        dk = jnp.zeros((rows, size), jnp.float32)
        dv = jnp.zeros((rows, size), jnp.float32)
        for j in (2, 3, 0, 1, 4):
            queries, grads = query_side(h, j)
            share, delta = get_rows(fin_own.at[slot] if j == 4 else fin_in.at[j, h])
            weights = (p_kept[slot, j] * (share * inv_kept[slot, j])).astype(jnp.bfloat16)
            ds = (weights.astype(jnp.float32) * (dp_kept[slot, j] - delta)).astype(jnp.bfloat16)
            dv += dot(weights, grads, NN)
            dk += dot(ds, queries, NN)
            dq = dot(keys_t, ds, NN) * scale
            if j == 4:
                dq_own[h] = dq
            else:
                ret_out[j, h] = dq.astype(jnp.bfloat16)
        dk_out[0, 0, :, columns(h)] = (dk * scale).astype(jnp.bfloat16)
        dv_out[0, 0, :, columns(h)] = dv.astype(jnp.bfloat16)
        for f in order:
            @pl.when(faces[f][1])
            def _(f=f):
                face_copy(ret_out, ret_in, ret_send, ret_recv, h, f).start()

    def query_step(h):
        for f in order:
            @pl.when(faces[f][1])
            def _(f=f):
                arrival(ret_in, ret_send, ret_recv, h, f).wait_recv()
        total = dq_own[h]
        for f in range(4):
            total += ret_in[f, h].astype(jnp.float32)
        dq_out[0, 0, :, columns(h)] = total.T.astype(jnp.bfloat16)

    def step(i, carry):
        @pl.when(i < HEADS)
        def _():
            score_step(i)

        @pl.when(jnp.logical_and(i >= NORM_LAG, i < HEADS + NORM_LAG))
        def _():
            norm_step(i - NORM_LAG)

        @pl.when(jnp.logical_and(i >= GRAD_LAG, i < HEADS + GRAD_LAG))
        def _():
            grad_step(i - GRAD_LAG)

        @pl.when(i + AHEAD < HEADS)
        def _():
            send_near(i + AHEAD)

        @pl.when(i >= QUERY_LAG)
        def _():
            query_step(i - QUERY_LAG)

        return carry

    lax.fori_loop(0, HEADS + QUERY_LAG, step, 0)

    for f in range(4):
        @pl.when(faces[f][1])
        def _(f=f):
            for out, send in ((near, near_send), (stat_out, stat_send), (fin_out, fin_send), (ret_out, ret_send)):
                pltpu.make_async_remote_copy(
                    out.at[f], out.at[f], send.at[f], near_recv.at[f, 0], device_id=faces[f][0], device_id_type=MESH
                ).wait_send()


def hand_over(a, b, c, x, y, z, sem):
    copies = [pltpu.make_async_copy(p, q, sem.at[i]) for i, (p, q) in enumerate(((a, x), (b, y), (c, z)))]
    for copy in copies:
        copy.start()
    for copy in copies:
        copy.wait()


def solution(mesh):
    span_time, span_space = mesh.shape["tm"], mesh.shape["space"]

    def per_device(query_tiles, key_tiles, value_tiles, cotangent, pair_table):
        shape = query_tiles.shape
        rows, width = shape[2], shape[3]
        size = width // HEADS
        out = jax.ShapeDtypeStruct(shape, jnp.bfloat16)
        kept = pltpu.VMEM(shape, jnp.bfloat16)
        half, full = jnp.bfloat16, jnp.float32
        dma = pltpu.SemaphoreType.DMA
        results = pl.pallas_call(
            functools.partial(kernel, span_time, span_space, rows, size),
            out_shape=(kept, kept, kept),
            in_specs=[pl.BlockSpec(memory_space=pltpu.HBM)] * 5,
            out_specs=[pl.BlockSpec(memory_space=pltpu.VMEM)] * 3,
            scratch_shapes=[
                pltpu.SMEM((3, span_time, span_space), jnp.int32),
                pltpu.VMEM((rows, width), half),
                pltpu.VMEM((rows, width), half),
                pltpu.VMEM((rows, width), half),
                pltpu.VMEM((rows, width), half),
                pltpu.VMEM((4, HEADS, 2, rows, size), half),
                pltpu.VMEM((SLOTS, 5, rows, rows), full),
                pltpu.VMEM((SLOTS, 5, rows, rows), full),
                pltpu.VMEM((SLOTS, 5, 1, rows), full),
                pltpu.VMEM((SLOTS, 4, rows // 2), full),
                pltpu.VMEM((4, HEADS, 4, rows // 2), full),
                pltpu.VMEM((4, HEADS, 4, rows // 2), full),
                pltpu.VMEM((SLOTS, 4, rows // 2), full),
                pltpu.VMEM((4, HEADS, 4, rows // 2), full),
                pltpu.VMEM((4, HEADS, 4, rows // 2), full),
                pltpu.VMEM((4, HEADS, size, rows), half),
                pltpu.VMEM((4, HEADS, size, rows), half),
                pltpu.VMEM((HEADS, size, rows), full),
                dma((5,)),
            ]
            + [dma((4,)), dma((4, ROUNDS))] * 4,
            compiler_params=pltpu.CompilerParams(
                collective_id=0, has_side_effects=True, vmem_limit_bytes=58 << 20
            ),
            cost_estimate=pl.CostEstimate(
                flops=5 * 5 * 2 * rows * rows * width, bytes_accessed=14 * rows * width, transcendentals=5 * HEADS * rows * rows
            ),
        )(pair_table.transpose(2, 0, 1), query_tiles, key_tiles, value_tiles, cotangent)
        return pl.pallas_call(
            hand_over,
            out_shape=(out, out, out),
            in_specs=[pl.BlockSpec(memory_space=pltpu.VMEM)] * 3,
            out_specs=[pl.BlockSpec(memory_space=pl.ANY)] * 3,
            scratch_shapes=[dma((3,))],
            compiler_params=pltpu.CompilerParams(vmem_limit_bytes=1 << 20),
        )(*results)

    tile = P("tm", "space", None, None)
    return jax.shard_map(
        per_device, mesh=mesh, in_specs=(tile, tile, tile, tile, P()), out_specs=(tile, tile, tile), check_vma=False
    )
```

```python
import functools
import math

import jax
import jax.numpy as jnp
from jax import lax
from jax.experimental import pallas as pl
from jax.experimental.pallas import tpu as pltpu
from jax.sharding import PartitionSpec as P

HEADS = 12
NORM_LAG, GRAD_LAG, QUERY_LAG = 3, 6, 9
SLOTS = GRAD_LAG + 1
ROUNDS = 7
AHEAD = 4
FAR = -1e30
RING = 4
MESH = pl.DeviceIdType.MESH
OPPOSITE = (1, 0, 3, 2)
NT = (((1,), (1,)), ((), ()))
NN = (((1,), (0,)), ((), ()))


def dot(a, b, dims):
    return lax.dot_general(a, b, dims, preferred_element_type=jnp.float32)


def kernel(
    span_time, span_space, ring, rows, size,
    table_hbm, q_hbm, k_hbm, v_hbm, g_hbm,
    dq_out, dk_out, dv_out,
    table, q_own, k_own, v_own, g_own, near, p_kept, dp_kept, inv_kept,
    own_note, note_out, note_in,
    ret_out, ret_in, dq_own,
    load_sem, near_send, near_recv, note_send, note_recv, ret_send, ret_recv,
):
    t = lax.axis_index("tm")
    s = lax.axis_index("space")
    faces = (
        ((t - 1, s), t > 0, -span_space),
        ((t + 1, s), t < span_time - 1, span_space),
        ((t, s - 1), s > 0, -1),
        ((t, s + 1), s < span_space - 1, 1),
    )
    order = (2, 3, 0, 1)
    longer = jnp.logical_and(lax.rem(s, ring) == ring - 1, faces[3][1])
    turns = (
        (3, longer),
        (2, faces[2][1]),
        (3, jnp.logical_and(faces[3][1], jnp.logical_not(longer))),
        (0, faces[0][1]),
        (1, faces[1][1]),
    )
    scale = size ** (-0.5)
    to_exp2 = scale * math.log2(math.e)

    loads = [
        pltpu.make_async_copy(src.at[0, 0], dst, load_sem.at[i])
        for i, (src, dst) in enumerate(((q_hbm, q_own), (k_hbm, k_own), (v_hbm, v_own), (g_hbm, g_own)))
    ]
    loads.append(pltpu.make_async_copy(table_hbm, table, load_sem.at[4]))
    for load in loads:
        load.start()

    barrier = pltpu.get_barrier_semaphore()
    for device, there, _ in faces:
        @pl.when(there)
        def _(device=device):
            pl.semaphore_signal(barrier, 1, device_id=device, device_id_type=MESH)
    pl.semaphore_wait(barrier, sum(there.astype(jnp.int32) for _, there, _ in faces))

    def columns(h):
        return pl.ds(pl.multiple_of(h * size, size), size)

    def near_copies(h, f):
        return [
            pltpu.make_async_remote_copy(
                src.at[0, 0, :, columns(h)], near.at[OPPOSITE[f], h, u],
                near_send.at[f], near_recv.at[OPPOSITE[f], lax.rem(h, ROUNDS)],
                device_id=faces[f][0], device_id_type=MESH,
            )
            for u, src in enumerate((q_hbm, g_hbm))
        ]

    def face_copy(out, arrived, send, recv, h, f):
        return pltpu.make_async_remote_copy(
            out.at[f, h], arrived.at[OPPOSITE[f], h], send.at[f], recv.at[OPPOSITE[f], lax.rem(h, ROUNDS)],
            device_id=faces[f][0], device_id_type=MESH,
        )

    def arrival(arrived, send, recv, h, f):
        return pltpu.make_async_remote_copy(
            arrived.at[f, h], arrived.at[f, h], send.at[f], recv.at[f, lax.rem(h, ROUNDS)],
            device_id=faces[f][0], device_id_type=MESH,
        )

    def send_near(h):
        for f, now in turns:
            @pl.when(now)
            def _(f=f):
                for copy in near_copies(h, f):
                    copy.start()

    def start_first(h, carry):
        send_near(h)
        return carry

    lax.fori_loop(0, AHEAD, start_first, 0)

    for f in range(4):
        @pl.when(jnp.logical_not(faces[f][1]))
        def _(f=f):
            def clear(h, carry):
                near[f, h] = jnp.zeros((2, rows, size), jnp.bfloat16)
                ret_in[f, h] = jnp.zeros((size, rows), jnp.bfloat16)
                return carry

            lax.fori_loop(0, HEADS, clear, 0)
            note_in[f] = jnp.zeros(note_in.shape[1:], jnp.float32)

    for load in loads:
        load.wait()

    number = t * span_space + s
    first, second = table[1, t, s], table[2, t, s]
    listed = [
        jnp.logical_or(first == number + by, second == number + by) for _, _, by in faces
    ]

    def get_row(note, row):
        return jnp.concatenate([note[row : row + 1, :], note[row + 1 : row + 2, :]], axis=1)

    def put_row(note, row, value):
        half = rows // 2
        note[row : row + 1, :] = value[:, :half]
        note[row + 1 : row + 2, :] = value[:, half:]

    def query_side(h, j):
        if j == 4:
            return q_own[:, columns(h)], g_own[:, columns(h)]
        return near[j, h, 0], near[j, h, 1]

    def score_step(h):
        slot = lax.rem(h, SLOTS)
        keys, values = k_own[:, columns(h)], v_own[:, columns(h)]
        def one(j):
            queries, grads = query_side(h, j)
            scores = dot(keys, queries, NT)
            peak = jnp.max(scores, axis=0, keepdims=True)
            p = jnp.exp2((scores - peak) * to_exp2)
            dp = dot(values, grads, NT)
            p_kept[slot, j] = p
            dp_kept[slot, j] = dp
            total = jnp.sum(p, axis=0, keepdims=True)
            inverse = 1.0 / total
            delta = jnp.sum(p * dp, axis=0, keepdims=True) * inverse
            inv_kept[slot, j] = inverse
            note = own_note.at[slot] if j == 4 else note_out.at[j, h]
            put_row(note, 0, peak * to_exp2 + jnp.log2(total))
            put_row(note, 2, delta)

        one(4)
        for f in order:
            @pl.when(faces[f][1])
            def _(f=f):
                arrival(near, near_send, near_recv, h, f).wait_recv()
        for j in order:
            one(j)

    def norm_step(h):
        slot = lax.rem(h, SLOTS)
        norms, deltas = [], []
        for f in range(4):
            norms.append(jnp.where(listed[f], note_in[f, h, 0:2, :], FAR))
            deltas.append(jnp.where(listed[f], note_in[f, h, 2:4, :], 0.0))
        norms.append(own_note[slot, 0:2, :])
        deltas.append(own_note[slot, 2:4, :])
        peak = functools.reduce(jnp.maximum, norms)
        shares = [jnp.exp2(norm - peak) for norm in norms]
        inverse = 1.0 / functools.reduce(jnp.add, shares)
        shares = [share * inverse for share in shares]
        delta = functools.reduce(jnp.add, [a * b for a, b in zip(shares, deltas)])
        for f in range(5):
            note = own_note.at[slot] if f == 4 else note_out.at[f, h + NORM_LAG]
            note[4:6, :] = shares[f]
            note[6:8, :] = delta

    def grad_step(h):
        slot = lax.rem(h, SLOTS)
        keys_t = k_own[:, columns(h)].T
        kept = []

        def one(j):
            note = own_note.at[slot] if j == 4 else note_in.at[j, h + NORM_LAG]
            share, delta = get_row(note, 4), get_row(note, 6)
            weights = (p_kept[slot, j] * (share * inv_kept[slot, j])).astype(jnp.bfloat16)
            ds = (weights.astype(jnp.float32) * (dp_kept[slot, j] - delta)).astype(jnp.bfloat16)
            kept.append((j, weights, ds))
            return dot(keys_t, ds, NN) * scale

        for j in order:
            ret_out[j, h] = one(j).astype(jnp.bfloat16)
        for f, now in turns:
            @pl.when(now)
            def _(f=f):
                face_copy(ret_out, ret_in, ret_send, ret_recv, h, f).start()
        dq_own[h] = one(4)
        dk = jnp.zeros((rows, size), jnp.float32)
        dv = jnp.zeros((rows, size), jnp.float32)
        for j, weights, ds in kept:
            queries, grads = query_side(h, j)
            dv += dot(weights, grads, NN)
            dk += dot(ds, queries, NN)
        dk_out[0, 0, :, columns(h)] = (dk * scale).astype(jnp.bfloat16)
        dv_out[0, 0, :, columns(h)] = dv.astype(jnp.bfloat16)

    def query_step(h):
        for f in order:
            @pl.when(faces[f][1])
            def _(f=f):
                arrival(ret_in, ret_send, ret_recv, h, f).wait_recv()
        total = dq_own[h]
        for f in range(4):
            total += ret_in[f, h].astype(jnp.float32)
        dq_out[0, 0, :, columns(h)] = total.astype(jnp.bfloat16).T

    def step(i, carry):
        @pl.when(i < HEADS)
        def _():
            score_step(i)

        @pl.when(jnp.logical_and(i >= NORM_LAG, i < HEADS + 2 * NORM_LAG))
        def _():
            for f in order:
                @pl.when(faces[f][1])
                def _(f=f):
                    arrival(note_in, note_send, note_recv, i - NORM_LAG, f).wait_recv()

        @pl.when(jnp.logical_and(i >= NORM_LAG, i < HEADS + NORM_LAG))
        def _():
            norm_step(i - NORM_LAG)

        @pl.when(i < HEADS + NORM_LAG)
        def _():
            for f, now in turns:
                @pl.when(now)
                def _(f=f):
                    face_copy(note_out, note_in, note_send, note_recv, i, f).start()

        @pl.when(jnp.logical_and(i >= GRAD_LAG, i < HEADS + GRAD_LAG))
        def _():
            grad_step(i - GRAD_LAG)

        @pl.when(i + AHEAD < HEADS)
        def _():
            send_near(i + AHEAD)

        @pl.when(i >= QUERY_LAG)
        def _():
            query_step(i - QUERY_LAG)

        return carry

    lax.fori_loop(0, HEADS + QUERY_LAG, step, 0)

    for f in range(4):
        @pl.when(faces[f][1])
        def _(f=f):
            for out, send in ((near, near_send), (note_out, note_send), (ret_out, ret_send)):
                pltpu.make_async_remote_copy(
                    out.at[f], out.at[f], send.at[f], near_recv.at[f, 0], device_id=faces[f][0], device_id_type=MESH
                ).wait_send()


def hand_over(a, b, c, x, y, z, sem):
    copies = [pltpu.make_async_copy(p, q, sem.at[i]) for i, (p, q) in enumerate(((a, x), (b, y), (c, z)))]
    for copy in copies:
        copy.start()
    for copy in copies:
        copy.wait()


def solution(mesh):
    span_time, span_space = mesh.shape["tm"], mesh.shape["space"]

    def per_device(query_tiles, key_tiles, value_tiles, cotangent, pair_table):
        shape = query_tiles.shape
        rows, width = shape[2], shape[3]
        size = width // HEADS
        out = jax.ShapeDtypeStruct(shape, jnp.bfloat16)
        kept = pltpu.VMEM(shape, jnp.bfloat16)
        half, full = jnp.bfloat16, jnp.float32
        dma = pltpu.SemaphoreType.DMA
        results = pl.pallas_call(
            functools.partial(kernel, span_time, span_space, RING, rows, size),
            out_shape=(kept, kept, kept),
            in_specs=[pl.BlockSpec(memory_space=pltpu.HBM)] * 5,
            out_specs=[pl.BlockSpec(memory_space=pltpu.VMEM)] * 3,
            scratch_shapes=[
                pltpu.SMEM((3, span_time, span_space), jnp.int32),
                pltpu.VMEM((rows, width), half),
                pltpu.VMEM((rows, width), half),
                pltpu.VMEM((rows, width), half),
                pltpu.VMEM((rows, width), half),
                pltpu.VMEM((4, HEADS, 2, rows, size), half),
                pltpu.VMEM((SLOTS, 5, rows, rows), full),
                pltpu.VMEM((SLOTS, 5, rows, rows), full),
                pltpu.VMEM((SLOTS, 5, 1, rows), full),
                pltpu.VMEM((SLOTS, 8, rows // 2), full),
                pltpu.VMEM((4, HEADS + NORM_LAG, 8, rows // 2), full),
                pltpu.VMEM((4, HEADS + NORM_LAG, 8, rows // 2), full),
                pltpu.VMEM((4, HEADS, size, rows), half),
                pltpu.VMEM((4, HEADS, size, rows), half),
                pltpu.VMEM((HEADS, size, rows), full),
                dma((5,)),
            ]
            + [dma((4,)), dma((4, ROUNDS))] * 3,
            compiler_params=pltpu.CompilerParams(
                collective_id=0, has_side_effects=True, vmem_limit_bytes=58 << 20
            ),
            cost_estimate=pl.CostEstimate(
                flops=5 * 5 * 2 * rows * rows * width, bytes_accessed=14 * rows * width, transcendentals=5 * HEADS * rows * rows
            ),
        )(pair_table.transpose(2, 0, 1), query_tiles, key_tiles, value_tiles, cotangent)
        return pl.pallas_call(
            hand_over,
            out_shape=(out, out, out),
            in_specs=[pl.BlockSpec(memory_space=pltpu.VMEM)] * 3,
            out_specs=[pl.BlockSpec(memory_space=pl.ANY)] * 3,
            scratch_shapes=[dma((3,))],
            compiler_params=pltpu.CompilerParams(vmem_limit_bytes=1 << 20),
        )(*results)

    tile = P("tm", "space", None, None)
    return jax.shard_map(
        per_device, mesh=mesh, in_specs=(tile, tile, tile, tile, P()), out_specs=(tile, tile, tile), check_vma=False
    )
```

```python
import functools
import math

import jax
import jax.numpy as jnp
from jax import lax
from jax.experimental import pallas as pl
from jax.experimental.pallas import tpu as pltpu
from jax.sharding import PartitionSpec as P

HEADS = 12
NORM_LAG, GRAD_LAG, QUERY_LAG = 3, 6, 9
SLOTS = GRAD_LAG + 1
ROUNDS = 7
AHEAD = 4
FAR = -1e30
RING = 4
MESH = pl.DeviceIdType.MESH
OPPOSITE = (1, 0, 3, 2)
NT = (((1,), (1,)), ((), ()))
NN = (((1,), (0,)), ((), ()))


def dot(a, b, dims):
    return lax.dot_general(a, b, dims, preferred_element_type=jnp.float32)


def kernel(
    span_time, span_space, ring, rows, size,
    table_hbm, q_hbm, k_hbm, v_hbm, g_hbm,
    dq_out, dk_out, dv_out,
    table, q_own, k_own, v_own, g_own, near, p_kept, dp_kept, inv_kept,
    own_note, note_out, note_in,
    ret_out, ret_in, dq_own,
    load_sem, near_send, near_recv, note_send, note_recv, ret_send, ret_recv,
):
    t = lax.axis_index("tm")
    s = lax.axis_index("space")
    faces = (
        ((t - 1, s), t > 0, -span_space),
        ((t + 1, s), t < span_time - 1, span_space),
        ((t, s - 1), s > 0, -1),
        ((t, s + 1), s < span_space - 1, 1),
    )
    order = (2, 3, 0, 1)
    longer = jnp.logical_and(lax.rem(s, ring) == ring - 1, faces[3][1])
    turns = (
        (3, longer),
        (2, faces[2][1]),
        (3, jnp.logical_and(faces[3][1], jnp.logical_not(longer))),
        (0, faces[0][1]),
        (1, faces[1][1]),
    )
    scale = size ** (-0.5)
    to_exp2 = scale * math.log2(math.e)

    loads = [
        pltpu.make_async_copy(src.at[0, 0], dst, load_sem.at[i])
        for i, (src, dst) in enumerate(((q_hbm, q_own), (k_hbm, k_own), (v_hbm, v_own), (g_hbm, g_own)))
    ]
    loads.append(pltpu.make_async_copy(table_hbm, table, load_sem.at[4]))
    for load in loads:
        load.start()

    barrier = pltpu.get_barrier_semaphore()
    for device, there, _ in reversed(faces):
        @pl.when(there)
        def _(device=device):
            pl.semaphore_signal(barrier, 1, device_id=device, device_id_type=MESH)
    pl.semaphore_wait(barrier, sum(there.astype(jnp.int32) for _, there, _ in faces))

    def columns(h):
        return pl.ds(pl.multiple_of(h * size, size), size)

    def near_copies(h, f):
        return [
            pltpu.make_async_remote_copy(
                src.at[0, 0, :, columns(h)], near.at[OPPOSITE[f], h, u],
                near_send.at[f], near_recv.at[OPPOSITE[f], lax.rem(h, ROUNDS)],
                device_id=faces[f][0], device_id_type=MESH,
            )
            for u, src in enumerate((q_hbm, g_hbm))
        ]

    def face_copy(out, arrived, send, recv, h, f):
        return pltpu.make_async_remote_copy(
            out.at[f, h], arrived.at[OPPOSITE[f], h], send.at[f], recv.at[OPPOSITE[f], lax.rem(h, ROUNDS)],
            device_id=faces[f][0], device_id_type=MESH,
        )

    def arrival(arrived, send, recv, h, f):
        return pltpu.make_async_remote_copy(
            arrived.at[f, h], arrived.at[f, h], send.at[f], recv.at[f, lax.rem(h, ROUNDS)],
            device_id=faces[f][0], device_id_type=MESH,
        )

    def send_near(h):
        for f, now in turns:
            @pl.when(now)
            def _(f=f):
                for copy in near_copies(h, f):
                    copy.start()

    def start_first(h, carry):
        send_near(h)
        return carry

    lax.fori_loop(0, AHEAD, start_first, 0)

    for f in range(4):
        @pl.when(jnp.logical_not(faces[f][1]))
        def _(f=f):
            def clear(h, carry):
                near[f, h] = jnp.zeros((2, rows, size), jnp.bfloat16)
                ret_in[f, h] = jnp.zeros((size, rows), jnp.bfloat16)
                return carry

            lax.fori_loop(0, HEADS, clear, 0)
            note_in[f] = jnp.zeros(note_in.shape[1:], jnp.float32)

    for load in loads:
        load.wait()

    number = t * span_space + s
    first, second = table[1, t, s], table[2, t, s]
    listed = [
        jnp.logical_and(there, jnp.logical_or(first == number + by, second == number + by))
        for _, there, by in faces
    ]

    def get_row(note, row):
        return jnp.concatenate([note[row : row + 1, :], note[row + 1 : row + 2, :]], axis=1)

    def put_row(note, row, value):
        half = rows // 2
        note[row : row + 1, :] = value[:, :half]
        note[row + 1 : row + 2, :] = value[:, half:]

    def query_side(h, j):
        if j == 4:
            return q_own[:, columns(h)], g_own[:, columns(h)]
        return near[j, h, 0], near[j, h, 1]

    def score_step(h):
        slot = lax.rem(h, SLOTS)
        keys, values = k_own[:, columns(h)], v_own[:, columns(h)]
        def one(j):
            queries, grads = query_side(h, j)
            scores = dot(keys, queries, NT)
            peak = jnp.max(scores, axis=0, keepdims=True)
            p = jnp.exp2((scores - peak) * to_exp2)
            dp = dot(values, grads, NT)
            p_kept[slot, j] = p
            dp_kept[slot, j] = dp
            total = jnp.sum(p, axis=0, keepdims=True)
            inverse = 1.0 / total
            delta = jnp.sum(p * dp, axis=0, keepdims=True) * inverse
            inv_kept[slot, j] = inverse
            note = own_note.at[slot] if j == 4 else note_out.at[j, h]
            put_row(note, 0, peak * to_exp2 + jnp.log2(total))
            put_row(note, 2, delta)

        one(4)
        for f in order:
            @pl.when(faces[f][1])
            def _(f=f):
                arrival(near, near_send, near_recv, h, f).wait_recv()
        for j in order:
            one(j)

    def norm_step(h):
        slot = lax.rem(h, SLOTS)
        norms, deltas = [], []
        for f in range(4):
            norms.append(jnp.where(listed[f], note_in[f, h, 0:2, :], FAR))
            deltas.append(jnp.where(listed[f], note_in[f, h, 2:4, :], 0.0))
        norms.append(own_note[slot, 0:2, :])
        deltas.append(own_note[slot, 2:4, :])
        peak = functools.reduce(jnp.maximum, norms)
        shares = [jnp.exp2(norm - peak) for norm in norms]
        inverse = 1.0 / functools.reduce(jnp.add, shares)
        shares = [share * inverse for share in shares]
        delta = functools.reduce(jnp.add, [a * b for a, b in zip(shares, deltas)])
        for f in range(5):
            note = own_note.at[slot] if f == 4 else note_out.at[f, h + NORM_LAG]
            note[4:6, :] = shares[f]
            note[6:8, :] = delta

    def grad_step(h):
        slot = lax.rem(h, SLOTS)
        keys_t = k_own[:, columns(h)].T
        kept = []

        def one(j):
            note = own_note.at[slot] if j == 4 else note_in.at[j, h + NORM_LAG]
            share, delta = get_row(note, 4), get_row(note, 6)
            weights = (p_kept[slot, j] * (share * inv_kept[slot, j])).astype(jnp.bfloat16)
            ds = (weights.astype(jnp.float32) * (dp_kept[slot, j] - delta)).astype(jnp.bfloat16)
            kept.append((j, weights, ds))
            return dot(keys_t, ds, NN) * scale

        for j in order:
            ret_out[j, h] = one(j).astype(jnp.bfloat16)
        for f, now in turns:
            @pl.when(now)
            def _(f=f):
                face_copy(ret_out, ret_in, ret_send, ret_recv, h, f).start()
        dq_own[h] = one(4)
        dk = jnp.zeros((rows, size), jnp.float32)
        dv = jnp.zeros((rows, size), jnp.float32)
        for j, weights, ds in kept:
            queries, grads = query_side(h, j)
            dv += dot(weights, grads, NN)
            dk += dot(ds, queries, NN)
        dk_out[0, 0, :, columns(h)] = (dk * scale).astype(jnp.bfloat16)
        dv_out[0, 0, :, columns(h)] = dv.astype(jnp.bfloat16)

    def query_step(h):
        for f in order:
            @pl.when(faces[f][1])
            def _(f=f):
                arrival(ret_in, ret_send, ret_recv, h, f).wait_recv()
        total = dq_own[h]
        for f in range(4):
            total += ret_in[f, h].astype(jnp.float32)
        dq_out[0, 0, :, columns(h)] = total.astype(jnp.bfloat16).T

    def step(i, carry):
        @pl.when(i < HEADS)
        def _():
            score_step(i)

        @pl.when(jnp.logical_and(i >= NORM_LAG, i < HEADS + 2 * NORM_LAG))
        def _():
            for f in order:
                @pl.when(faces[f][1])
                def _(f=f):
                    arrival(note_in, note_send, note_recv, i - NORM_LAG, f).wait_recv()

        @pl.when(jnp.logical_and(i >= NORM_LAG, i < HEADS + NORM_LAG))
        def _():
            norm_step(i - NORM_LAG)

        @pl.when(i < HEADS + NORM_LAG)
        def _():
            for f, now in turns:
                @pl.when(now)
                def _(f=f):
                    face_copy(note_out, note_in, note_send, note_recv, i, f).start()

        @pl.when(jnp.logical_and(i >= GRAD_LAG, i < HEADS + GRAD_LAG))
        def _():
            grad_step(i - GRAD_LAG)

        @pl.when(i + AHEAD < HEADS)
        def _():
            send_near(i + AHEAD)

        @pl.when(i >= QUERY_LAG)
        def _():
            query_step(i - QUERY_LAG)

        return carry

    lax.fori_loop(0, HEADS + QUERY_LAG, step, 0)

    for f in range(4):
        @pl.when(faces[f][1])
        def _(f=f):
            for out, send in ((near, near_send), (note_out, note_send), (ret_out, ret_send)):
                pltpu.make_async_remote_copy(
                    out.at[f], out.at[f], send.at[f], near_recv.at[f, 0], device_id=faces[f][0], device_id_type=MESH
                ).wait_send()


def hand_over(a, b, c, x, y, z, sem):
    copies = [pltpu.make_async_copy(p, q, sem.at[i]) for i, (p, q) in enumerate(((a, x), (b, y), (c, z)))]
    for copy in copies:
        copy.start()
    for copy in copies:
        copy.wait()


def solution(mesh):
    span_time, span_space = mesh.shape["tm"], mesh.shape["space"]

    def per_device(query_tiles, key_tiles, value_tiles, cotangent, pair_table):
        shape = query_tiles.shape
        rows, width = shape[2], shape[3]
        size = width // HEADS
        out = jax.ShapeDtypeStruct(shape, jnp.bfloat16)
        kept = pltpu.VMEM(shape, jnp.bfloat16)
        half, full = jnp.bfloat16, jnp.float32
        dma = pltpu.SemaphoreType.DMA
        results = pl.pallas_call(
            functools.partial(kernel, span_time, span_space, RING, rows, size),
            out_shape=(kept, kept, kept),
            in_specs=[pl.BlockSpec(memory_space=pltpu.HBM)] * 5,
            out_specs=[pl.BlockSpec(memory_space=pltpu.VMEM)] * 3,
            scratch_shapes=[
                pltpu.SMEM((3, span_time, span_space), jnp.int32),
                pltpu.VMEM((rows, width), half),
                pltpu.VMEM((rows, width), half),
                pltpu.VMEM((rows, width), half),
                pltpu.VMEM((rows, width), half),
                pltpu.VMEM((4, HEADS, 2, rows, size), half),
                pltpu.VMEM((SLOTS, 5, rows, rows), full),
                pltpu.VMEM((SLOTS, 5, rows, rows), full),
                pltpu.VMEM((SLOTS, 5, 1, rows), full),
                pltpu.VMEM((SLOTS, 8, rows // 2), full),
                pltpu.VMEM((4, HEADS + NORM_LAG, 8, rows // 2), full),
                pltpu.VMEM((4, HEADS + NORM_LAG, 8, rows // 2), full),
                pltpu.VMEM((4, HEADS, size, rows), half),
                pltpu.VMEM((4, HEADS, size, rows), half),
                pltpu.VMEM((HEADS, size, rows), full),
                dma((5,)),
            ]
            + [dma((4,)), dma((4, ROUNDS))] * 3,
            compiler_params=pltpu.CompilerParams(
                collective_id=0, has_side_effects=True, vmem_limit_bytes=58 << 20
            ),
            cost_estimate=pl.CostEstimate(
                flops=5 * 5 * 2 * rows * rows * width, bytes_accessed=14 * rows * width, transcendentals=5 * HEADS * rows * rows
            ),
        )(pair_table.transpose(2, 0, 1), query_tiles, key_tiles, value_tiles, cotangent)
        return pl.pallas_call(
            hand_over,
            out_shape=(out, out, out),
            in_specs=[pl.BlockSpec(memory_space=pltpu.VMEM)] * 3,
            out_specs=[pl.BlockSpec(memory_space=pl.ANY)] * 3,
            scratch_shapes=[dma((3,))],
            compiler_params=pltpu.CompilerParams(vmem_limit_bytes=1 << 20),
        )(*results)

    tile = P("tm", "space", None, None)
    return jax.shard_map(
        per_device, mesh=mesh, in_specs=(tile, tile, tile, tile, P()), out_specs=(tile, tile, tile), check_vma=False
    )
```

```python
import functools
import math

import jax
import jax.numpy as jnp
from jax import lax
from jax.experimental import pallas as pl
from jax.experimental.pallas import tpu as pltpu
from jax.sharding import PartitionSpec as P

HEADS = 12
NORM_LAG, GRAD_LAG, QUERY_LAG = 3, 6, 9
SLOTS = GRAD_LAG + 1
ROUNDS = 7
AHEAD = 4
FAR = -1e30
RING = 4
MESH = pl.DeviceIdType.MESH
OPPOSITE = (1, 0, 3, 2)
NT = (((1,), (1,)), ((), ()))
NN = (((1,), (0,)), ((), ()))


def dot(a, b, dims):
    return lax.dot_general(a, b, dims, preferred_element_type=jnp.float32)


def kernel(
    span_time, span_space, ring, rows, size,
    table_hbm, q_hbm, k_hbm, v_hbm, g_hbm,
    dq_out, dk_out, dv_out,
    table, q_own, k_own, v_own, g_own, near, p_kept, dp_kept, inv_kept,
    own_note, note_out, note_in,
    ret_out, ret_in, dq_own,
    load_sem, near_send, near_recv, note_send, note_recv, ret_send, ret_recv,
):
    t = lax.axis_index("tm")
    s = lax.axis_index("space")
    faces = (
        ((t - 1, s), t > 0, -span_space),
        ((t + 1, s), t < span_time - 1, span_space),
        ((t, s - 1), s > 0, -1),
        ((t, s + 1), s < span_space - 1, 1),
    )
    order = (2, 3, 0, 1)
    longer = jnp.logical_and(lax.rem(s, ring) == ring - 1, faces[3][1])
    turns = (
        (3, longer),
        (2, faces[2][1]),
        (3, jnp.logical_and(faces[3][1], jnp.logical_not(longer))),
        (0, faces[0][1]),
        (1, faces[1][1]),
    )
    scale = size ** (-0.5)
    to_exp2 = scale * math.log2(math.e)

    loads = [
        pltpu.make_async_copy(src.at[0, 0], dst, load_sem.at[i])
        for i, (src, dst) in enumerate(((q_hbm, q_own), (k_hbm, k_own), (v_hbm, v_own), (g_hbm, g_own)))
    ]
    loads.append(pltpu.make_async_copy(table_hbm, table, load_sem.at[4]))
    for load in loads:
        load.start()

    barrier = pltpu.get_barrier_semaphore()
    for device, there, _ in reversed(faces):
        @pl.when(there)
        def _(device=device):
            pl.semaphore_signal(barrier, 1, device_id=device, device_id_type=MESH)
    pl.semaphore_wait(barrier, sum(there.astype(jnp.int32) for _, there, _ in faces))

    def columns(h):
        return pl.ds(pl.multiple_of(h * size, size), size)

    def near_copies(h, f):
        return [
            pltpu.make_async_remote_copy(
                src.at[0, 0, :, columns(h)], near.at[OPPOSITE[f], h, u],
                near_send.at[f], near_recv.at[OPPOSITE[f], lax.rem(h, ROUNDS)],
                device_id=faces[f][0], device_id_type=MESH,
            )
            for u, src in enumerate((q_hbm, g_hbm))
        ]

    def face_copy(out, arrived, send, recv, h, f):
        return pltpu.make_async_remote_copy(
            out.at[f, h], arrived.at[OPPOSITE[f], h], send.at[f], recv.at[OPPOSITE[f], lax.rem(h, ROUNDS)],
            device_id=faces[f][0], device_id_type=MESH,
        )

    def arrival(arrived, send, recv, h, f):
        return pltpu.make_async_remote_copy(
            arrived.at[f, h], arrived.at[f, h], send.at[f], recv.at[f, lax.rem(h, ROUNDS)],
            device_id=faces[f][0], device_id_type=MESH,
        )

    def note_copy(i, f, first, count):
        rows_used = pl.ds(first, count)
        return pltpu.make_async_remote_copy(
            note_out.at[f, i, rows_used], note_in.at[OPPOSITE[f], i, rows_used],
            note_send.at[f], note_recv.at[OPPOSITE[f], lax.rem(i, ROUNDS)],
            device_id=faces[f][0], device_id_type=MESH,
        )

    def note_arrival(i, f, first, count):
        arrived = note_in.at[f, i, pl.ds(first, count)]
        return pltpu.make_async_remote_copy(
            arrived, arrived, note_send.at[f], note_recv.at[f, lax.rem(i, ROUNDS)],
            device_id=faces[f][0], device_id_type=MESH,
        )

    def used_rows(i):
        return (
            (i < NORM_LAG, 0, 4),
            (jnp.logical_and(i >= NORM_LAG, i < HEADS), 0, 8),
            (i >= HEADS, 4, 4),
        )

    def send_near(h):
        for f, now in turns:
            @pl.when(now)
            def _(f=f):
                for copy in near_copies(h, f):
                    copy.start()

    def start_first(h, carry):
        send_near(h)
        return carry

    lax.fori_loop(0, AHEAD, start_first, 0)

    for f in range(4):
        @pl.when(jnp.logical_not(faces[f][1]))
        def _(f=f):
            def clear(h, carry):
                near[f, h] = jnp.zeros((2, rows, size), jnp.bfloat16)
                ret_in[f, h] = jnp.zeros((size, rows), jnp.bfloat16)
                return carry

            lax.fori_loop(0, HEADS, clear, 0)
            note_in[f] = jnp.zeros(note_in.shape[1:], jnp.float32)

    for load in loads:
        load.wait()

    number = t * span_space + s
    first, second = table[1, t, s], table[2, t, s]
    listed = [
        jnp.logical_and(there, jnp.logical_or(first == number + by, second == number + by))
        for _, there, by in faces
    ]

    def get_row(note, row):
        return jnp.concatenate([note[row : row + 1, :], note[row + 1 : row + 2, :]], axis=1)

    def put_row(note, row, value):
        half = rows // 2
        note[row : row + 1, :] = value[:, :half]
        note[row + 1 : row + 2, :] = value[:, half:]

    def query_side(h, j):
        if j == 4:
            return q_own[:, columns(h)], g_own[:, columns(h)]
        return near[j, h, 0], near[j, h, 1]

    def score_step(h):
        slot = lax.rem(h, SLOTS)
        keys, values = k_own[:, columns(h)], v_own[:, columns(h)]
        def one(j):
            queries, grads = query_side(h, j)
            scores = dot(keys, queries, NT)
            peak = jnp.max(scores, axis=0, keepdims=True)
            p = jnp.exp2((scores - peak) * to_exp2)
            dp = dot(values, grads, NT)
            p_kept[slot, j] = p
            dp_kept[slot, j] = dp
            total = jnp.sum(p, axis=0, keepdims=True)
            inverse = 1.0 / total
            delta = jnp.sum(p * dp, axis=0, keepdims=True) * inverse
            inv_kept[slot, j] = inverse
            note = own_note.at[slot] if j == 4 else note_out.at[j, h]
            put_row(note, 0, peak * to_exp2 + jnp.log2(total))
            put_row(note, 2, delta)

        one(4)
        for f in order:
            @pl.when(faces[f][1])
            def _(f=f):
                arrival(near, near_send, near_recv, h, f).wait_recv()
        for j in order:
            one(j)

    def norm_step(h):
        slot = lax.rem(h, SLOTS)
        norms, deltas = [], []
        for f in range(4):
            norms.append(jnp.where(listed[f], note_in[f, h, 0:2, :], FAR))
            deltas.append(jnp.where(listed[f], note_in[f, h, 2:4, :], 0.0))
        norms.append(own_note[slot, 0:2, :])
        deltas.append(own_note[slot, 2:4, :])
        peak = functools.reduce(jnp.maximum, norms)
        shares = [jnp.exp2(norm - peak) for norm in norms]
        inverse = 1.0 / functools.reduce(jnp.add, shares)
        shares = [share * inverse for share in shares]
        delta = functools.reduce(jnp.add, [a * b for a, b in zip(shares, deltas)])
        for f in range(5):
            note = own_note.at[slot] if f == 4 else note_out.at[f, h + NORM_LAG]
            note[4:6, :] = shares[f]
            note[6:8, :] = delta

    def grad_step(h):
        slot = lax.rem(h, SLOTS)
        keys_t = k_own[:, columns(h)].T
        kept = []

        def one(j):
            note = own_note.at[slot] if j == 4 else note_in.at[j, h + NORM_LAG]
            share, delta = get_row(note, 4), get_row(note, 6)
            weights = (p_kept[slot, j] * (share * inv_kept[slot, j])).astype(jnp.bfloat16)
            ds = (weights.astype(jnp.float32) * (dp_kept[slot, j] - delta)).astype(jnp.bfloat16)
            kept.append((j, weights, ds))
            return dot(keys_t, ds, NN) * scale

        for j in order:
            ret_out[j, h] = one(j).astype(jnp.bfloat16)
        for f, now in turns:
            @pl.when(now)
            def _(f=f):
                face_copy(ret_out, ret_in, ret_send, ret_recv, h, f).start()
        dq_own[h] = one(4)
        dk = jnp.zeros((rows, size), jnp.float32)
        dv = jnp.zeros((rows, size), jnp.float32)
        for j, weights, ds in kept:
            queries, grads = query_side(h, j)
            dv += dot(weights, grads, NN)
            dk += dot(ds, queries, NN)
        dk_out[0, 0, :, columns(h)] = (dk * scale).astype(jnp.bfloat16)
        dv_out[0, 0, :, columns(h)] = dv.astype(jnp.bfloat16)

    def query_step(h):
        for f in order:
            @pl.when(faces[f][1])
            def _(f=f):
                arrival(ret_in, ret_send, ret_recv, h, f).wait_recv()
        total = dq_own[h]
        for f in range(4):
            total += ret_in[f, h].astype(jnp.float32)
        dq_out[0, 0, :, columns(h)] = total.astype(jnp.bfloat16).T

    def step(i, carry):
        @pl.when(i < HEADS)
        def _():
            score_step(i)

        @pl.when(jnp.logical_and(i >= NORM_LAG, i < HEADS + 2 * NORM_LAG))
        def _():
            for now, first, count in used_rows(i - NORM_LAG):
                @pl.when(now)
                def _(first=first, count=count):
                    for f in order:
                        @pl.when(faces[f][1])
                        def _(f=f):
                            note_arrival(i - NORM_LAG, f, first, count).wait_recv()

        @pl.when(jnp.logical_and(i >= NORM_LAG, i < HEADS + NORM_LAG))
        def _():
            norm_step(i - NORM_LAG)

        @pl.when(i < HEADS + NORM_LAG)
        def _():
            for used, first, count in used_rows(i):
                @pl.when(used)
                def _(first=first, count=count):
                    for f, now in turns:
                        @pl.when(now)
                        def _(f=f):
                            note_copy(i, f, first, count).start()

        @pl.when(jnp.logical_and(i >= GRAD_LAG, i < HEADS + GRAD_LAG))
        def _():
            grad_step(i - GRAD_LAG)

        @pl.when(i + AHEAD < HEADS)
        def _():
            send_near(i + AHEAD)

        @pl.when(i >= QUERY_LAG)
        def _():
            query_step(i - QUERY_LAG)

        return carry

    lax.fori_loop(0, HEADS + QUERY_LAG, step, 0)

    for f in range(4):
        @pl.when(faces[f][1])
        def _(f=f):
            for out, send in ((near, near_send), (note_out, note_send), (ret_out, ret_send)):
                pltpu.make_async_remote_copy(
                    out.at[f, pl.ds(0, HEADS)], out.at[f, pl.ds(0, HEADS)], send.at[f], near_recv.at[f, 0], device_id=faces[f][0], device_id_type=MESH
                ).wait_send()


def hand_over(a, b, c, x, y, z, sem):
    copies = [pltpu.make_async_copy(p, q, sem.at[i]) for i, (p, q) in enumerate(((a, x), (b, y), (c, z)))]
    for copy in copies:
        copy.start()
    for copy in copies:
        copy.wait()


def solution(mesh):
    span_time, span_space = mesh.shape["tm"], mesh.shape["space"]

    def per_device(query_tiles, key_tiles, value_tiles, cotangent, pair_table):
        shape = query_tiles.shape
        rows, width = shape[2], shape[3]
        size = width // HEADS
        out = jax.ShapeDtypeStruct(shape, jnp.bfloat16)
        kept = pltpu.VMEM(shape, jnp.bfloat16)
        half, full = jnp.bfloat16, jnp.float32
        dma = pltpu.SemaphoreType.DMA
        results = pl.pallas_call(
            functools.partial(kernel, span_time, span_space, RING, rows, size),
            out_shape=(kept, kept, kept),
            in_specs=[pl.BlockSpec(memory_space=pltpu.HBM)] * 5,
            out_specs=[pl.BlockSpec(memory_space=pltpu.VMEM)] * 3,
            scratch_shapes=[
                pltpu.SMEM((3, span_time, span_space), jnp.int32),
                pltpu.VMEM((rows, width), half),
                pltpu.VMEM((rows, width), half),
                pltpu.VMEM((rows, width), half),
                pltpu.VMEM((rows, width), half),
                pltpu.VMEM((4, HEADS, 2, rows, size), half),
                pltpu.VMEM((SLOTS, 5, rows, rows), full),
                pltpu.VMEM((SLOTS, 5, rows, rows), full),
                pltpu.VMEM((SLOTS, 5, 1, rows), full),
                pltpu.VMEM((SLOTS, 8, rows // 2), full),
                pltpu.VMEM((4, HEADS + NORM_LAG, 8, rows // 2), full),
                pltpu.VMEM((4, HEADS + NORM_LAG, 8, rows // 2), full),
                pltpu.VMEM((4, HEADS, size, rows), half),
                pltpu.VMEM((4, HEADS, size, rows), half),
                pltpu.VMEM((HEADS, size, rows), full),
                dma((5,)),
            ]
            + [dma((4,)), dma((4, ROUNDS))] * 3,
            compiler_params=pltpu.CompilerParams(
                collective_id=0, has_side_effects=True, vmem_limit_bytes=58 << 20
            ),
            cost_estimate=pl.CostEstimate(
                flops=5 * 5 * 2 * rows * rows * width, bytes_accessed=14 * rows * width, transcendentals=5 * HEADS * rows * rows
            ),
        )(pair_table.transpose(2, 0, 1), query_tiles, key_tiles, value_tiles, cotangent)
        return pl.pallas_call(
            hand_over,
            out_shape=(out, out, out),
            in_specs=[pl.BlockSpec(memory_space=pltpu.VMEM)] * 3,
            out_specs=[pl.BlockSpec(memory_space=pl.ANY)] * 3,
            scratch_shapes=[dma((3,))],
            compiler_params=pltpu.CompilerParams(vmem_limit_bytes=1 << 20),
        )(*results)

    tile = P("tm", "space", None, None)
    return jax.shard_map(
        per_device, mesh=mesh, in_specs=(tile, tile, tile, tile, P()), out_specs=(tile, tile, tile), check_vma=False
    )
```

```python
import functools
import math

import jax
import jax.numpy as jnp
from jax import lax
from jax.experimental import pallas as pl
from jax.experimental.pallas import tpu as pltpu
from jax.sharding import PartitionSpec as P

HEADS = 12
NORM_LAG, GRAD_LAG, QUERY_LAG = 3, 6, 9
SLOTS = GRAD_LAG + 1
ROUNDS = 7
AHEAD = 4
FAR = -1e30
RING = 4
MESH = pl.DeviceIdType.MESH
OPPOSITE = (1, 0, 3, 2)
NT = (((1,), (1,)), ((), ()))
NN = (((1,), (0,)), ((), ()))


def dot(a, b, dims):
    return lax.dot_general(a, b, dims, preferred_element_type=jnp.float32)


def kernel(
    span_time, span_space, ring, rows, size,
    table_hbm, q_hbm, k_hbm, v_hbm, g_hbm,
    dq_out, dk_out, dv_out,
    table, q_own, k_own, v_own, g_own, near, p_kept, dp_kept, inv_kept,
    own_note, note_out, note_in,
    ret_out, ret_in, dq_own,
    load_sem, near_send, near_recv, note_send, note_recv, ret_send, ret_recv,
):
    t = lax.axis_index("tm")
    s = lax.axis_index("space")
    faces = (
        ((t - 1, s), t > 0, -span_space),
        ((t + 1, s), t < span_time - 1, span_space),
        ((t, s - 1), s > 0, -1),
        ((t, s + 1), s < span_space - 1, 1),
    )
    order = (2, 3, 0, 1)
    longer = jnp.logical_and(lax.rem(s, ring) == ring - 1, faces[3][1])
    turns = (
        (3, longer),
        (2, faces[2][1]),
        (3, jnp.logical_and(faces[3][1], jnp.logical_not(longer))),
        (0, faces[0][1]),
        (1, faces[1][1]),
    )
    scale = size ** (-0.5)
    to_exp2 = scale * math.log2(math.e)

    loads = [
        pltpu.make_async_copy(src.at[0, 0], dst, load_sem.at[i])
        for i, (src, dst) in enumerate(((q_hbm, q_own), (k_hbm, k_own), (v_hbm, v_own), (g_hbm, g_own)))
    ]
    loads.append(pltpu.make_async_copy(table_hbm, table, load_sem.at[4]))
    for load in loads:
        load.start()

    barrier = pltpu.get_barrier_semaphore()
    for device, there, _ in reversed(faces):
        @pl.when(there)
        def _(device=device):
            pl.semaphore_signal(barrier, 1, device_id=device, device_id_type=MESH)
    pl.semaphore_wait(barrier, sum(there.astype(jnp.int32) for _, there, _ in faces))

    def columns(h):
        return pl.ds(pl.multiple_of(h * size, size), size)

    def near_copies(h, f):
        return [
            pltpu.make_async_remote_copy(
                src.at[0, 0, :, columns(h)], near.at[OPPOSITE[f], h, u],
                near_send.at[f], near_recv.at[OPPOSITE[f], lax.rem(h, ROUNDS)],
                device_id=faces[f][0], device_id_type=MESH,
            )
            for u, src in enumerate((q_hbm, g_hbm))
        ]

    def face_copy(out, arrived, send, recv, h, f):
        return pltpu.make_async_remote_copy(
            out.at[f, h], arrived.at[OPPOSITE[f], h], send.at[f], recv.at[OPPOSITE[f], lax.rem(h, ROUNDS)],
            device_id=faces[f][0], device_id_type=MESH,
        )

    def arrival(arrived, send, recv, h, f):
        return pltpu.make_async_remote_copy(
            arrived.at[f, h], arrived.at[f, h], send.at[f], recv.at[f, lax.rem(h, ROUNDS)],
            device_id=faces[f][0], device_id_type=MESH,
        )

    def send_near(h, turns=turns):
        for f, now in turns:
            @pl.when(now)
            def _(f=f):
                for copy in near_copies(h, f):
                    copy.start()

    def start_first(some):
        def start(h, carry):
            send_near(h, some)
            return carry

        return start

    send_near(0)
    lax.fori_loop(1, AHEAD, start_first(turns[:3]), 0)
    lax.fori_loop(1, AHEAD, start_first(turns[3:]), 0)

    for f in range(4):
        @pl.when(jnp.logical_not(faces[f][1]))
        def _(f=f):
            def clear(h, carry):
                near[f, h] = jnp.zeros((2, rows, size), jnp.bfloat16)
                ret_in[f, h] = jnp.zeros((size, rows), jnp.bfloat16)
                return carry

            lax.fori_loop(0, HEADS, clear, 0)
            note_in[f] = jnp.zeros(note_in.shape[1:], jnp.float32)

    for load in loads:
        load.wait()

    number = t * span_space + s
    first, second = table[1, t, s], table[2, t, s]
    listed = [
        jnp.logical_and(there, jnp.logical_or(first == number + by, second == number + by))
        for _, there, by in faces
    ]

    def get_row(note, row):
        return jnp.concatenate([note[row : row + 1, :], note[row + 1 : row + 2, :]], axis=1)

    def put_row(note, row, value):
        half = rows // 2
        note[row : row + 1, :] = value[:, :half]
        note[row + 1 : row + 2, :] = value[:, half:]

    def query_side(h, j):
        if j == 4:
            return q_own[:, columns(h)], g_own[:, columns(h)]
        return near[j, h, 0], near[j, h, 1]

    def score_step(h):
        slot = lax.rem(h, SLOTS)
        keys, values = k_own[:, columns(h)], v_own[:, columns(h)]
        def one(j):
            queries, grads = query_side(h, j)
            scores = dot(keys, queries, NT)
            peak = jnp.max(scores, axis=0, keepdims=True)
            p = jnp.exp2((scores - peak) * to_exp2)
            dp = dot(values, grads, NT)
            p_kept[slot, j] = p
            dp_kept[slot, j] = dp
            total = jnp.sum(p, axis=0, keepdims=True)
            inverse = 1.0 / total
            delta = jnp.sum(p * dp, axis=0, keepdims=True) * inverse
            inv_kept[slot, j] = inverse
            note = own_note.at[slot] if j == 4 else note_out.at[j, h]
            put_row(note, 0, peak * to_exp2 + jnp.log2(total))
            put_row(note, 2, delta)

        one(4)
        for f in order:
            @pl.when(faces[f][1])
            def _(f=f):
                arrival(near, near_send, near_recv, h, f).wait_recv()
        for j in order:
            one(j)

    def norm_step(h):
        slot = lax.rem(h, SLOTS)
        norms, deltas = [], []
        for f in range(4):
            norms.append(jnp.where(listed[f], note_in[f, h, 0:2, :], FAR))
            deltas.append(jnp.where(listed[f], note_in[f, h, 2:4, :], 0.0))
        norms.append(own_note[slot, 0:2, :])
        deltas.append(own_note[slot, 2:4, :])
        peak = functools.reduce(jnp.maximum, norms)
        shares = [jnp.exp2(norm - peak) for norm in norms]
        inverse = 1.0 / functools.reduce(jnp.add, shares)
        shares = [share * inverse for share in shares]
        delta = functools.reduce(jnp.add, [a * b for a, b in zip(shares, deltas)])
        for f in range(5):
            note = own_note.at[slot] if f == 4 else note_out.at[f, h + NORM_LAG]
            note[4:6, :] = shares[f]
            note[6:8, :] = delta

    def grad_step(h):
        slot = lax.rem(h, SLOTS)
        keys_t = k_own[:, columns(h)].T
        kept = []

        def one(j):
            note = own_note.at[slot] if j == 4 else note_in.at[j, h + NORM_LAG]
            share, delta = get_row(note, 4), get_row(note, 6)
            weights = (p_kept[slot, j] * (share * inv_kept[slot, j])).astype(jnp.bfloat16)
            ds = (weights.astype(jnp.float32) * (dp_kept[slot, j] - delta)).astype(jnp.bfloat16)
            kept.append((j, weights, ds))
            return dot(keys_t, ds, NN) * scale

        for j in order:
            ret_out[j, h] = one(j).astype(jnp.bfloat16)
        for f, now in turns:
            @pl.when(now)
            def _(f=f):
                face_copy(ret_out, ret_in, ret_send, ret_recv, h, f).start()
        dq_own[h] = one(4)
        dk = jnp.zeros((rows, size), jnp.float32)
        dv = jnp.zeros((rows, size), jnp.float32)
        for j, weights, ds in kept:
            queries, grads = query_side(h, j)
            dv += dot(weights, grads, NN)
            dk += dot(ds, queries, NN)
        dk_out[0, 0, :, columns(h)] = (dk * scale).astype(jnp.bfloat16)
        dv_out[0, 0, :, columns(h)] = dv.astype(jnp.bfloat16)

    def query_step(h):
        for f in order:
            @pl.when(faces[f][1])
            def _(f=f):
                arrival(ret_in, ret_send, ret_recv, h, f).wait_recv()
        total = dq_own[h]
        for f in range(4):
            total += ret_in[f, h].astype(jnp.float32)
        dq_out[0, 0, :, columns(h)] = total.astype(jnp.bfloat16).T

    def step(i, carry):
        @pl.when(i < HEADS)
        def _():
            score_step(i)

        @pl.when(jnp.logical_and(i >= NORM_LAG, i < HEADS + 2 * NORM_LAG))
        def _():
            for f in order:
                @pl.when(faces[f][1])
                def _(f=f):
                    arrival(note_in, note_send, note_recv, i - NORM_LAG, f).wait_recv()

        @pl.when(jnp.logical_and(i >= NORM_LAG, i < HEADS + NORM_LAG))
        def _():
            norm_step(i - NORM_LAG)

        @pl.when(i < HEADS + NORM_LAG)
        def _():
            for f, now in turns:
                @pl.when(now)
                def _(f=f):
                    face_copy(note_out, note_in, note_send, note_recv, i, f).start()

        @pl.when(jnp.logical_and(i >= GRAD_LAG, i < HEADS + GRAD_LAG))
        def _():
            grad_step(i - GRAD_LAG)

        @pl.when(i + AHEAD < HEADS)
        def _():
            send_near(i + AHEAD)

        @pl.when(i >= QUERY_LAG)
        def _():
            query_step(i - QUERY_LAG)

        return carry

    lax.fori_loop(0, HEADS + QUERY_LAG, step, 0)

    for f in range(4):
        @pl.when(faces[f][1])
        def _(f=f):
            for out, send in ((near, near_send), (note_out, note_send), (ret_out, ret_send)):
                pltpu.make_async_remote_copy(
                    out.at[f], out.at[f], send.at[f], near_recv.at[f, 0], device_id=faces[f][0], device_id_type=MESH
                ).wait_send()


def hand_over(a, b, c, x, y, z, sem):
    copies = [pltpu.make_async_copy(p, q, sem.at[i]) for i, (p, q) in enumerate(((a, x), (b, y), (c, z)))]
    for copy in copies:
        copy.start()
    for copy in copies:
        copy.wait()


def solution(mesh):
    span_time, span_space = mesh.shape["tm"], mesh.shape["space"]

    def per_device(query_tiles, key_tiles, value_tiles, cotangent, pair_table):
        shape = query_tiles.shape
        rows, width = shape[2], shape[3]
        size = width // HEADS
        out = jax.ShapeDtypeStruct(shape, jnp.bfloat16)
        kept = pltpu.VMEM(shape, jnp.bfloat16)
        half, full = jnp.bfloat16, jnp.float32
        dma = pltpu.SemaphoreType.DMA
        results = pl.pallas_call(
            functools.partial(kernel, span_time, span_space, RING, rows, size),
            out_shape=(kept, kept, kept),
            in_specs=[pl.BlockSpec(memory_space=pltpu.HBM)] * 5,
            out_specs=[pl.BlockSpec(memory_space=pltpu.VMEM)] * 3,
            scratch_shapes=[
                pltpu.SMEM((3, span_time, span_space), jnp.int32),
                pltpu.VMEM((rows, width), half),
                pltpu.VMEM((rows, width), half),
                pltpu.VMEM((rows, width), half),
                pltpu.VMEM((rows, width), half),
                pltpu.VMEM((4, HEADS, 2, rows, size), half),
                pltpu.VMEM((SLOTS, 5, rows, rows), full),
                pltpu.VMEM((SLOTS, 5, rows, rows), full),
                pltpu.VMEM((SLOTS, 5, 1, rows), full),
                pltpu.VMEM((SLOTS, 8, rows // 2), full),
                pltpu.VMEM((4, HEADS + NORM_LAG, 8, rows // 2), full),
                pltpu.VMEM((4, HEADS + NORM_LAG, 8, rows // 2), full),
                pltpu.VMEM((4, HEADS, size, rows), half),
                pltpu.VMEM((4, HEADS, size, rows), half),
                pltpu.VMEM((HEADS, size, rows), full),
                dma((5,)),
            ]
            + [dma((4,)), dma((4, ROUNDS))] * 3,
            compiler_params=pltpu.CompilerParams(
                collective_id=0, has_side_effects=True, vmem_limit_bytes=58 << 20
            ),
            cost_estimate=pl.CostEstimate(
                flops=5 * 5 * 2 * rows * rows * width, bytes_accessed=14 * rows * width, transcendentals=5 * HEADS * rows * rows
            ),
        )(pair_table.transpose(2, 0, 1), query_tiles, key_tiles, value_tiles, cotangent)
        return pl.pallas_call(
            hand_over,
            out_shape=(out, out, out),
            in_specs=[pl.BlockSpec(memory_space=pltpu.VMEM)] * 3,
            out_specs=[pl.BlockSpec(memory_space=pl.ANY)] * 3,
            scratch_shapes=[dma((3,))],
            compiler_params=pltpu.CompilerParams(vmem_limit_bytes=1 << 20),
        )(*results)

    tile = P("tm", "space", None, None)
    return jax.shard_map(
        per_device, mesh=mesh, in_specs=(tile, tile, tile, tile, P()), out_specs=(tile, tile, tile), check_vma=False
    )
```
